32 devices in a mesh: groups: 2 (over x), chan: 16 (over z, y, core).
Axes of the slice: x: 2, y: 2, z: 4, core: 2. Of those that a mesh axis runs over, the one named last changes fastest.
Arguments:
- snapshots: bfloat16 [4, 4096, 4096], P('groups', 'chan'), parts along dimension 0, may hold values from -6 to 6
- freq_bins: int32 [512], replicated, may hold values from 1 to 2047
- mode_shapes: bfloat16 [8, 64, 4096], P(None, None, 'chan'), may hold values from -8 to 8
- mode_counts: int32 [8], replicated, may hold values from 16 to 64
- wavenumbers: float32 [8, 64, 512], replicated, may hold values from 20 to 200
- source_modes: float32 [8, 64, 128], replicated, may hold values from -5 to 5
- segment_owner: int32 [4], replicated, may hold values from 0 to 7
Outputs:
- localization: float32 [32, 128], P(('groups', 'chan')), parts along dimension 0
The draws below stay inside these ranges and needn't reach their ends.
There are 2 independent parts, one for each index of `groups`. The reference program is written for one: setup_inputs(seed, part) draws one part's arguments, and reference() takes and returns one part's arrays. A program takes and returns all parts, laid end to end along the dimension named above; an argument that names none is the same for every part. Nothing has to cross between parts.
All inputs are finite; a program needn't handle non-finite values.
Results may differ from the reference program's by a relative error of at most 0.0019.
Values may be sent and summed in bfloat16 or wider, within the bound.
A program may use at most 128 MiB of HBM per device.

```python
import math
import jax
import jax.numpy as jnp
from jax import lax

CHANNELS = 4096
NS = 4096
F = 512
L = 2
SEG = 8
M = 64
NZ = 128
RPB = 4
RB = 4


def draw_mode_shapes(key, part):
    key = jax.random.fold_in(key, 11)
    own_key = jax.random.fold_in(key, 1)
    common_key = jax.random.fold_in(key, 2)
    position = jnp.arange(CHANNELS, dtype=jnp.float32) / CHANNELS
    slope = 0.5 + 1.5 * position
    base = jnp.clip(jax.random.normal(own_key, (SEG, M, CHANNELS), jnp.float32), -2.5, 2.5)
    common = 0.6 * jnp.clip(jax.random.normal(common_key, (SEG, 1, CHANNELS), jnp.float32), -2.5, 2.5)
    values = (base + common) * slope[None, None, :]
    return jnp.clip(values, -8.0, 8.0).astype(jnp.bfloat16)


def with_ends(drawn, key, least, largest):
    dims = drawn.shape
    spot = [jax.random.randint(jax.random.fold_in(key, axis), (), 0, dims[axis]) for axis in range(len(dims))]
    drawn = drawn.at[tuple(spot)].set(least)
    longest = dims.index(max(dims))
    spot[longest] = (spot[longest] + 1) % dims[longest]
    return drawn.at[tuple(spot)].set(largest)


def block_scale(key, dims, pieces, low, top_value):
    factor_of, own = 1.0, jax.random.fold_in(key, 6)
    for dim, blocks in pieces:
        draws = jnp.exp(jax.random.uniform(jax.random.fold_in(own, dim), (blocks,), jnp.float32, low / len(pieces), top_value / len(pieces)))
        factor_of = factor_of * jnp.repeat(draws, dims[dim] // blocks).reshape([-1 if axis == dim else 1 for axis in range(len(dims))])
    return factor_of


def noise(key, extent, width, bound, split=(), kind=jnp.bfloat16):
    drawn = width * jax.random.normal(key, extent, jnp.float32)
    if split:
        drawn = drawn * block_scale(key, extent, split, -0.22, 0.18)
    return jnp.clip(drawn, -bound, bound).astype(kind)


def setup_inputs(seed: int = 0, part: int = 0) -> dict:
    arg_keys = jax.random.split(jax.random.key(seed), 8)
    part_keys = jax.random.split(jax.random.fold_in(arg_keys[7], part), 8)
    return {
        "snapshots": noise(part_keys[0], (L, CHANNELS, NS), 1.0, 6.0, ((1, 16),)),
        "freq_bins": with_ends(jax.random.randint(arg_keys[1], (F,), 1, NS // 2), jax.random.fold_in(arg_keys[1], 1), 1, (NS // 2) - 1).astype(jnp.int32),
        "mode_shapes": draw_mode_shapes(jax.random.fold_in(arg_keys[7], 71), part),
        "mode_counts": with_ends(jax.random.randint(arg_keys[3], (SEG,), M // 4, M + 1), jax.random.fold_in(arg_keys[3], 1), M // 4, M).astype(jnp.int32),
        "wavenumbers": jnp.clip(jnp.exp(jax.random.uniform(arg_keys[4], (SEG, M, F), jnp.float32, math.log(20.0), math.log(200.0))), 20.0, 200.0),
        "source_modes": noise(arg_keys[5], (SEG, M, NZ), 1.0, 5.0, (), jnp.float32),
        "segment_owner": with_ends(jax.random.randint(arg_keys[6], (RB,), 0, SEG), jax.random.fold_in(arg_keys[6], 1), 0, SEG - 1).astype(jnp.int32),
    }


range_start = 1.0
range_step = 0.01

def dft_table(freq_bins, samples):
    sample_ids = jnp.arange(samples, dtype=jnp.int32)
    residue = freq_bins[:, None] * sample_ids[None, :] % samples
    angles = residue.astype(jnp.float32) * (2.0 * jnp.pi / samples)
    return jnp.stack([jnp.cos(angles), -jnp.sin(angles)]).astype(jnp.bfloat16)

def surface_terms(proj_rounded, gram_rounded, traces, waves, source_modes, mode_counts, segment_owner, ranges_per_block, freq_total):
    segs, modes, depths = source_modes.shape
    freqs = proj_rounded.shape[0]
    snaps = proj_rounded.shape[2]
    blocks = segment_owner.shape[0]
    highest = lax.Precision.HIGHEST
    active = (jnp.arange(modes, dtype=jnp.int32)[None, :] < mode_counts[:, None]).astype(jnp.float32)
    masked = source_modes * active[:, :, None]
    select = (segment_owner[:, None] == jnp.arange(segs, dtype=jnp.int32)[None, :]).astype(jnp.float32)
    wave_blocks = jnp.einsum('bs,smf->bfm', select, waves, precision=highest)
    mode_blocks = jnp.einsum('bs,smz->bzm', select, masked, precision=highest)
    proj_blocks = jnp.einsum('bs,fclsm->bfclm', select, proj_rounded.astype(jnp.float32), precision=highest).astype(jnp.bfloat16)
    gram_blocks = jnp.einsum('bs,smn->bmn', select, gram_rounded.astype(jnp.float32), precision=highest).astype(jnp.bfloat16)

    def one_block(items):
        block_id, wave_block, mode_block, proj_block, gram_block = items
        range_ids = block_id * ranges_per_block + jnp.arange(ranges_per_block, dtype=jnp.int32)
        ranges = range_start + range_step * range_ids.astype(jnp.float32)
        phases = wave_block[:, None, :] * ranges[None, :, None]
        amplitude = mode_block[None, None, :, :] / jnp.sqrt(phases)[:, :, None, :]
        replica_real = amplitude * jnp.cos(phases)[:, :, None, :]
        replica_imag = amplitude * jnp.sin(phases)[:, :, None, :]
        cells = ranges_per_block * depths
        replica = jnp.concatenate([replica_real, replica_imag], axis=-1).reshape(freqs, cells, 2 * modes).astype(jnp.bfloat16)
        proj_real = proj_block[:, 0]
        proj_imag = proj_block[:, 1]
        upper = jnp.concatenate([proj_real, proj_imag], axis=1)
        lower = jnp.concatenate([proj_imag, -proj_real], axis=1)
        coupling = jnp.concatenate([upper, lower], axis=-1)
        beams = jnp.einsum('fcm,fkm->fck', replica.astype(jnp.float32), coupling.astype(jnp.float32))
        powers = lax.optimization_barrier(jnp.sum(beams * beams, axis=-1))
        halves = replica.reshape(freqs, cells, 2, modes).astype(jnp.float32)
        mapped = jnp.einsum('fcpm,mn->fcpn', halves, gram_block.astype(jnp.float32))
        weight_norm = lax.optimization_barrier(jnp.sum(halves * mapped, axis=(2, 3)))
        bartlett = powers / (snaps * traces[:, None] * weight_norm)
        return (lax.optimization_barrier(jnp.sum(bartlett, axis=0)) / freq_total).reshape(ranges_per_block, depths)
    block_ids = jnp.arange(blocks, dtype=jnp.int32)
    parts = lax.map(one_block, (block_ids, wave_blocks, mode_blocks, proj_blocks, gram_blocks))
    return parts.reshape(blocks * ranges_per_block, depths)

def reference(snapshots, freq_bins, mode_shapes, mode_counts, wavenumbers, source_modes, segment_owner):
    table_values = dft_table(freq_bins, NS)
    spectra = jnp.einsum('cft,lht->cflh', table_values.astype(jnp.float32), snapshots.astype(jnp.float32)).astype(jnp.bfloat16)
    spectra_wide = spectra.astype(jnp.float32)
    traces = lax.optimization_barrier(jnp.sum(spectra_wide * spectra_wide, axis=(0, 2, 3)))
    shapes_wide = mode_shapes.astype(jnp.float32)
    projections = jnp.einsum('cflh,smh->fclsm', spectra_wide, shapes_wide)
    proj_rounded = projections.astype(jnp.bfloat16)
    gram = jnp.einsum('smh,snh->smn', shapes_wide, shapes_wide)
    gram_rounded = gram.astype(jnp.bfloat16)
    surface = surface_terms(proj_rounded, gram_rounded, traces, wavenumbers, source_modes, mode_counts, segment_owner, RPB, F)
    return surface / jnp.max(surface)
```

```python
import functools
import math

import jax
import jax.numpy as jnp
from jax import lax
from jax.experimental import pallas as pl
from jax.experimental.pallas import tpu as pltpu
from jax.sharding import PartitionSpec as P

F = 512
RPB = 4


range_start = 1.0
range_step = 0.01


def dft_table(freq_bins, samples):
    sample_ids = jnp.arange(samples, dtype=jnp.int32)
    residue = freq_bins[:, None] * sample_ids[None, :] % samples
    angles = residue.astype(jnp.float32) * (2.0 * jnp.pi / samples)
    return jnp.stack([jnp.cos(angles), -jnp.sin(angles)]).astype(jnp.bfloat16)


def surface_terms(
    proj_flat,
    gram_rounded,
    traces,
    waves,
    source_modes,
    mode_counts,
    segment_owner,
    ranges_per_block,
    freq_total,
):
    segs, modes, depths = source_modes.shape
    freqs = proj_flat.shape[0]
    snaps = proj_flat.shape[2]
    highest = lax.Precision.HIGHEST
    proj_four = proj_flat.reshape(freqs, 2, snaps, segs, modes)
    proj_real = proj_four[:, 0]
    proj_imag = proj_four[:, 1]
    upper = jnp.concatenate([proj_real, proj_imag], axis=-1)
    lower = jnp.concatenate([proj_imag, -proj_real], axis=-1)
    coupling = jnp.concatenate([upper, lower], axis=1)
    coupling = jnp.transpose(coupling, (2, 0, 1, 3)).astype(jnp.float32)
    zero_block = jnp.zeros_like(gram_rounded)
    gram_double = jnp.concatenate(
        [
            jnp.concatenate([gram_rounded, zero_block], axis=2),
            jnp.concatenate([zero_block, gram_rounded], axis=2),
        ],
        axis=1,
    ).astype(jnp.float32)
    active = (jnp.arange(modes, dtype=jnp.int32)[None, :] < mode_counts[:, None]).astype(
        jnp.float32
    )
    masked = jnp.transpose(source_modes * active[:, :, None], (0, 2, 1))
    mode_double = jnp.concatenate([masked, masked], axis=-1)
    wave_t = jnp.transpose(waves, (0, 2, 1))
    wave_double = jnp.concatenate([wave_t, wave_t], axis=-1)
    lanes = jnp.arange(2 * modes, dtype=jnp.int32) < modes
    seg_ids = jnp.arange(segs, dtype=jnp.int32)
    blocks = segment_owner.shape[0]

    def one_block(items):
        block_id, owner = items
        pick = (seg_ids == owner).astype(jnp.float32)
        wave_block = jnp.einsum("s,sfm->fm", pick, wave_double, precision=highest)
        mode_block = jnp.einsum("s,szm->zm", pick, mode_double, precision=highest)
        coupling_block = jnp.einsum("s,sfkm->fkm", pick, coupling, precision=highest).astype(
            jnp.bfloat16
        )
        gram_block = jnp.einsum("s,smn->mn", pick, gram_double, precision=highest).astype(
            jnp.bfloat16
        )
        range_ids = block_id * ranges_per_block + jnp.arange(ranges_per_block, dtype=jnp.int32)
        ranges = range_start + range_step * range_ids.astype(jnp.float32)
        phases = wave_block[:, None, :] * ranges[None, :, None]
        trig = jnp.where(lanes[None, None, :], jnp.cos(phases), jnp.sin(phases))
        amplitude = mode_block[None, None, :, :] / jnp.sqrt(phases)[:, :, None, :]
        cells = ranges_per_block * depths
        replica = (
            (amplitude * trig[:, :, None, :]).reshape(freqs, cells, 2 * modes).astype(jnp.bfloat16)
        )
        beams = jnp.einsum(
            "fkm,fcm->fkc", coupling_block, replica, preferred_element_type=jnp.float32
        )
        powers = jnp.sum(beams * beams, axis=1)
        mapped = jnp.einsum("fcm,mn->fcn", replica, gram_block, preferred_element_type=jnp.float32)
        weight_norm = jnp.sum(replica.astype(jnp.float32) * mapped, axis=-1)
        bartlett = powers / (snaps * traces[:, None] * weight_norm)
        return (jnp.sum(bartlett, axis=0) / freq_total).reshape(ranges_per_block, depths)

    block_ids = jnp.arange(blocks, dtype=jnp.int32)
    parts = lax.map(one_block, (block_ids, segment_owner))
    return parts.reshape(blocks * ranges_per_block, depths)


def per_device_plain(
    snapshots, freq_bins, mode_shapes, mode_counts, wavenumbers, source_modes, segment_owner
):
    devices_chan = lax.axis_size("chan")
    samples = snapshots.shape[2]
    segs = mode_shapes.shape[0]
    modes = mode_shapes.shape[1]
    local_freqs = F // devices_chan
    table_values = dft_table(freq_bins, samples)
    spectra = jnp.einsum(
        "cft,lht->cflh", table_values, snapshots, preferred_element_type=jnp.float32
    ).astype(jnp.bfloat16)
    moved = lax.all_to_all(spectra, "chan", split_axis=1, concat_axis=3, tiled=True)
    traces = jnp.sum(jnp.square(moved.astype(jnp.float32)), axis=(0, 2, 3))
    piece = lax.all_gather(mode_shapes, "chan", axis=2, tiled=True)
    flat_piece = piece.reshape(segs * modes, piece.shape[2])
    projections = jnp.einsum("cflh,kh->fclk", moved, flat_piece, preferred_element_type=jnp.float32)
    proj_rounded = projections.astype(jnp.bfloat16)
    local_gram = jnp.einsum(
        "smh,snh->smn", mode_shapes, mode_shapes, preferred_element_type=jnp.float32
    )
    gram = lax.psum(local_gram.reshape(segs, modes * modes), "chan")
    gram_rounded = gram.reshape(segs, modes, modes).astype(jnp.bfloat16)
    first_freq = lax.axis_index("chan") * local_freqs
    local_waves = lax.dynamic_slice_in_dim(wavenumbers, first_freq, local_freqs, 2)
    partial_surface = surface_terms(
        proj_rounded,
        gram_rounded,
        traces,
        local_waves,
        source_modes,
        mode_counts,
        segment_owner,
        RPB,
        F,
    )
    own_rows = partial_surface.shape[0] // devices_chan
    total_surface = lax.psum(partial_surface, "chan")
    highest_value = jnp.max(total_surface)
    own_surface = lax.dynamic_slice_in_dim(
        total_surface, lax.axis_index("chan") * own_rows, own_rows, 0
    )
    return own_surface / highest_value


LANES = 128
MESH = pl.DeviceIdType.MESH
HIGHEST = lax.Precision.HIGHEST


def sincos_small(x):
    y = x * x
    sine = x + x * y * (
        -1.6666667e-1 + y * (8.3333333e-3 + y * (-1.9841270e-4 + y * 2.7557319e-6))
    )
    cosine = 1.0 + y * (
        -0.5 + y * (4.1666667e-2 + y * (-1.3888889e-3 + y * (2.4801587e-5 - y * 2.7557319e-7)))
    )
    return sine, cosine


def turn(quadrant, sine, cosine):
    odd = (quadrant & 1) == 1
    c = jnp.where(odd, sine, cosine)
    s = jnp.where(odd, cosine, sine)
    return (
        jnp.where((quadrant & 2) != 0, -s, s),
        jnp.where(((quadrant + 1) & 2) != 0, -c, c),
    )


def sincos_bins(q, samples):
    quarter = samples // 4
    q = q & (samples - 1)
    quadrant = (q + quarter // 2) // quarter
    x = (q - quadrant * quarter).astype(jnp.float32) * (2.0 * math.pi / samples)
    return turn(quadrant, *sincos_small(x))


def sincos_wide(x):
    n = jnp.floor(x * (2.0 / math.pi) + 0.5)
    y = ((x - n * 1.5703125) - n * 4.837512969970703125e-4) - n * 7.54978995489188216e-8
    return turn(n.astype(jnp.int32), *sincos_small(y))


def fused_kernel(
    devices,
    freq_ref,
    snaps_hbm,
    modes_ref,
    phases_ref,
    source_ref,
    out_ref,
    snaps,
    table,
    cos_a,
    sin_a,
    cos_b,
    sin_b,
    proj_send,
    proj_recv,
    trace_send,
    trace_recv,
    gram_part,
    gram_recv,
    gram_own,
    gram_full,
    terms_a,
    terms_b,
    surf_own,
    surf_recv,
    total_ref,
    load_sem,
    proj_ssem,
    proj_rsem,
    trace_ssem,
    trace_rsem,
    gram_ssem,
    gram_rsem,
    full_ssem,
    full_rsem,
    surf_ssem,
    surf_rsem,
):
    me = lax.axis_index("chan")
    snap_count, channels, samples = snaps_hbm.shape
    blocks, modes, depths = source_ref.shape
    columns = freq_ref.shape[1]
    width = table.shape[1]
    f32 = jnp.float32

    barrier = pltpu.get_barrier_semaphore()
    for step in range(1, devices):
        pl.semaphore_signal(
            barrier, inc=1, device_id={"chan": (me + step) % devices}, device_id_type=MESH
        )
    load = pltpu.make_async_copy(snaps_hbm, snaps, load_sem)
    load.start()

    def send(src, dst, ssem, rsem, peer):
        return pltpu.make_async_remote_copy(
            src_ref=src,
            dst_ref=dst,
            send_sem=ssem,
            recv_sem=rsem,
            device_id={"chan": peer},
            device_id_type=MESH,
        )

    shapes = modes_ref[...]
    inner = lax.dot_general(shapes, shapes, (((1,), (1,)), ((), ())), preferred_element_type=f32)
    low_half = lax.broadcasted_iota(jnp.int32, (modes, LANES), 1) < modes
    for pair in range(blocks // 2):
        base = pair * LANES
        gram_part[pair * modes : (pair + 1) * modes, :] = jnp.where(
            low_half,
            inner[base : base + modes, base : base + LANES],
            inner[base + modes : base + LANES, base : base + LANES],
        )
    pl.semaphore_wait(barrier, devices - 1)

    @pl.loop(1, devices)
    def _(step):
        peer = (me + step) % devices
        send(
            gram_part.at[pl.ds(pl.multiple_of(peer * 8, 8), 8), :],
            gram_recv.at[me],
            gram_ssem.at[peer],
            gram_rsem.at[me],
            peer,
        ).start()

    gram_recv[me] = gram_part[pl.ds(pl.multiple_of(me * 8, 8), 8), :]

    half = cos_a.shape[0]
    freqs = freq_ref[...]
    column = lax.broadcasted_iota(jnp.int32, (half, columns), 1)
    row = lax.broadcasted_iota(jnp.int32, (half, columns), 0)
    part_size = columns // devices // 2
    shift = ((column // part_size) & 1) * (samples // 4)
    sin_v, cos_v = sincos_bins(freqs * (row * half) + shift, samples)
    sin_a[...] = sin_v
    cos_a[...] = cos_v
    sin_v, cos_v = sincos_bins(freqs * row, samples)
    sin_b[...] = sin_v
    cos_b[...] = cos_v

    @pl.loop(1, devices)
    def _(step):
        peer = (me + step) % devices
        send(
            gram_part.at[pl.ds(0, 8), :],
            gram_recv.at[peer],
            gram_ssem.at[peer],
            gram_rsem.at[peer],
            peer,
        ).wait_recv()

    gram_own[...] = jnp.sum(gram_recv[...], axis=0)
    own_rows = pl.ds(pl.multiple_of(me * 8, 8), 8)
    gram_full[own_rows, :] = gram_own[...]

    @pl.loop(1, devices)
    def _(step):
        peer = (me + step) % devices
        send(
            gram_own, gram_full.at[own_rows, :], full_ssem.at[peer], full_rsem.at[me], peer
        ).start()

    load.wait()
    per_chunk = width // (columns // devices)
    chunk_count = columns // width
    wide_low = lax.broadcasted_iota(jnp.int32, (blocks * modes, LANES), 1) < LANES // 2
    thin_low = wide_low[:8]

    @pl.loop(0, chunk_count)
    def _(step):
        chunk = (me // per_chunk + 1 + step) % chunk_count
        cols = pl.ds(pl.multiple_of(chunk * width, width), width)
        cb = cos_b[:, cols]
        sb = sin_b[:, cols]

        @pl.loop(0, half, unroll=4)
        def _(a):
            ca = cos_a[pl.ds(a, 1), cols]
            sa = sin_a[pl.ds(a, 1), cols]
            table[pl.ds(pl.multiple_of(a * half, half), half), :] = (ca * cb - sa * sb).astype(
                jnp.bfloat16
            )

        parts = []
        sums = []
        for snap in range(snap_count):
            spectra = jnp.dot(snaps[snap], table[...], preferred_element_type=f32).astype(
                jnp.bfloat16
            )
            wide = spectra.astype(f32)
            sums.append(jnp.broadcast_to(jnp.sum(wide * wide, axis=0, keepdims=True), (8, width)))
            parts.append(jnp.dot(shapes, spectra, preferred_element_type=f32))
        for pair in range(per_chunk // 2):
            lanes = slice(pair * LANES, (pair + 1) * LANES)
            p0, p1 = parts[0][:, lanes], parts[1][:, lanes]
            t0, t1 = sums[0][:, lanes], sums[1][:, lanes]
            for side in range(2):
                dest = chunk * per_chunk + 2 * pair + side
                if side == 0:
                    message = jnp.where(wide_low, p0, pltpu.roll(p1, LANES // 2, 1))
                    trace = jnp.where(thin_low, t0, pltpu.roll(t1, LANES // 2, 1))
                else:
                    message = jnp.where(wide_low, pltpu.roll(p0, LANES // 2, 1), p1)
                    trace = jnp.where(thin_low, pltpu.roll(t0, LANES // 2, 1), t1)
                proj_send[dest] = message.astype(jnp.bfloat16)
                trace_send[dest] = trace

                @pl.when(dest != me)
                def _():
                    send(
                        proj_send.at[dest],
                        proj_recv.at[me],
                        proj_ssem.at[dest],
                        proj_rsem.at[me],
                        dest,
                    ).start()
                    send(
                        trace_send.at[dest],
                        trace_recv.at[me],
                        trace_ssem.at[dest],
                        trace_rsem.at[me],
                        dest,
                    ).start()

    proj_recv[me] = proj_send[me]
    trace_recv[me] = trace_send[me]

    @pl.loop(1, devices)
    def _(step):
        peer = (me + step) % devices
        send(
            gram_own,
            gram_full.at[pl.ds(pl.multiple_of(peer * 8, 8), 8), :],
            full_ssem.at[peer],
            full_rsem.at[peer],
            peer,
        ).wait_recv()

    gram = gram_full[...].astype(jnp.bfloat16).astype(f32)
    waves_sin = []
    waves_cos = []
    norms = []
    for block in range(blocks):
        phases = phases_ref[block]
        sine, cosine = sincos_wide(phases)
        scale = 1.0 / jnp.sqrt(phases)
        sine, cosine = sine * scale, cosine * scale
        waves_sin.append(sine)
        waves_cos.append(cosine)
        source = source_ref[block]
        rows = slice((block // 2) * modes, (block // 2 + 1) * modes)
        for m in range(modes):
            lane = (block % 2) * modes + m
            at = slice(m * modes, (m + 1) * modes)
            terms_a[at, :] = (cosine[m : m + 1] * cosine + sine[m : m + 1] * sine).astype(
                jnp.bfloat16
            )
            terms_b[at, :] = (
                gram[rows, lane : lane + 1] * (source[m : m + 1] * source)
            ).astype(jnp.bfloat16)
        norms.append(
            lax.dot_general(
                terms_a[...],
                terms_b[...],
                (((0,), (0,)), ((), ())),
                preferred_element_type=f32,
            )
        )

    @pl.loop(1, devices)
    def _(step):
        peer = (me + step) % devices
        send(
            proj_send.at[peer], proj_recv.at[peer], proj_ssem.at[peer], proj_rsem.at[peer], peer
        ).wait_recv()
        send(
            trace_send.at[peer],
            trace_recv.at[peer],
            trace_ssem.at[peer],
            trace_rsem.at[peer],
            peer,
        ).wait_recv()

    proj = proj_recv[0].astype(f32)
    for source_id in range(1, devices):
        proj = proj + proj_recv[source_id].astype(f32)
    proj = proj.astype(jnp.bfloat16)
    trace = jnp.sum(trace_recv[...], axis=0)
    quarter = LANES // 4
    trace = trace + pltpu.roll(trace, 2 * quarter, 1)
    trace = trace + pltpu.roll(trace, quarter, 1)
    level = (1.0 / jnp.sqrt(snap_count * trace))[:1]

    pick_in = lax.broadcasted_iota(jnp.int32, (LANES, 4 * LANES), 0)
    pick_out = lax.broadcasted_iota(jnp.int32, (LANES, 4 * LANES), 1)
    pick = (pick_in // quarter == pick_out // LANES) & (pick_in % quarter == pick_out % quarter)
    spread = jnp.dot(proj, pick.astype(f32).astype(jnp.bfloat16), preferred_element_type=f32)
    for block in range(blocks):
        sine, cosine = waves_sin[block] * level, waves_cos[block] * level
        rows = slice(block * modes, (block + 1) * modes)
        coupled = []
        for snap in range(snap_count):
            real = spread[rows, (2 * snap) * LANES : (2 * snap + 1) * LANES]
            imag = spread[rows, (2 * snap + 1) * LANES : (2 * snap + 2) * LANES]
            coupled.append(cosine * real + sine * imag)
            coupled.append(cosine * imag - sine * real)
        coupled = jnp.concatenate(coupled, axis=1)
        coupled_high = coupled.astype(jnp.bfloat16)
        coupled_low = (coupled - coupled_high.astype(f32)).astype(jnp.bfloat16)
        source = source_ref[block]
        source_high = source.astype(jnp.bfloat16)
        source_low = (source - source_high.astype(f32)).astype(jnp.bfloat16)
        beams = lax.dot_general(
            jnp.concatenate([coupled_high, coupled_low, coupled_high], axis=0),
            jnp.concatenate([source_high, source_high, source_low], axis=0),
            (((0,), (0,)), ((), ())),
            preferred_element_type=f32,
        )
        squares = beams * beams
        power = (
            squares[:LANES]
            + squares[LANES : 2 * LANES]
            + squares[2 * LANES : 3 * LANES]
            + squares[3 * LANES :]
        )
        ratio = power / norms[block]
        for j in range(4):
            surf_own[block * 4 + j : block * 4 + j + 1, :] = jnp.sum(
                ratio[j * quarter : (j + 1) * quarter], axis=0, keepdims=True
            )

    surf_recv[me] = surf_own[...]

    @pl.loop(1, devices)
    def _(step):
        peer = (me + step) % devices
        send(surf_own, surf_recv.at[me], surf_ssem.at[peer], surf_rsem.at[me], peer).start()

    @pl.loop(1, devices)
    def _(step):
        peer = (me + step) % devices
        send(surf_own, surf_recv.at[peer], surf_ssem.at[peer], surf_rsem.at[peer], peer).wait_recv()

    total = jnp.sum(surf_recv[...], axis=0) / (columns // 2)
    total_ref[...] = total
    out_ref[...] = total_ref[pl.ds(me, 1), :] / jnp.max(total)

    @pl.loop(1, devices)
    def _(step):
        peer = (me + step) % devices
        send(
            gram_part.at[pl.ds(pl.multiple_of(peer * 8, 8), 8), :],
            gram_recv.at[me],
            gram_ssem.at[peer],
            gram_rsem.at[me],
            peer,
        ).wait_send()
        send(
            gram_own, gram_full.at[own_rows, :], full_ssem.at[peer], full_rsem.at[me], peer
        ).wait_send()
        send(
            proj_send.at[peer], proj_recv.at[me], proj_ssem.at[peer], proj_rsem.at[me], peer
        ).wait_send()
        send(
            trace_send.at[peer], trace_recv.at[me], trace_ssem.at[peer], trace_rsem.at[me], peer
        ).wait_send()
        send(surf_own, surf_recv.at[me], surf_ssem.at[peer], surf_rsem.at[me], peer).wait_send()


def per_device_fused(
    snapshots, freq_bins, mode_shapes, mode_counts, wavenumbers, source_modes, segment_owner
):
    devices = lax.axis_size("chan")
    snap_count, channels, samples = snapshots.shape
    segs, modes, depths = source_modes.shape
    blocks = segment_owner.shape[0]
    freqs = freq_bins.shape[0]
    local_freqs = freqs // devices
    columns = 2 * freqs
    half = math.isqrt(samples)
    freq_columns = jnp.broadcast_to(
        freq_bins.reshape(devices, 1, local_freqs), (devices, 2, local_freqs)
    ).reshape(1, columns)
    shapes = jnp.take(mode_shapes, segment_owner, axis=0).reshape(blocks * modes, channels)
    active = jnp.arange(modes, dtype=jnp.int32)[None, :] < mode_counts[:, None]
    masked = jnp.take(source_modes * active[:, :, None], segment_owner, axis=0)
    first_freq = lax.axis_index("chan") * local_freqs
    waves = lax.dynamic_slice_in_dim(wavenumbers, first_freq, local_freqs, 2)
    waves = jnp.take(waves, segment_owner, axis=0)
    ranges = range_start + range_step * jnp.arange(blocks * RPB, dtype=jnp.float32)
    phases = waves[:, :, None, :] * ranges.reshape(blocks, 1, RPB, 1)
    phases = phases.reshape(blocks, modes, RPB * local_freqs)
    f32, bf16 = jnp.float32, jnp.bfloat16
    ranges_total = blocks * RPB
    dma = pltpu.SemaphoreType.DMA((devices,))
    vmem = pl.BlockSpec(memory_space=pltpu.VMEM)
    return pl.pallas_call(
        functools.partial(fused_kernel, devices),
        out_shape=jax.ShapeDtypeStruct((1, depths), f32),
        in_specs=[vmem, pl.BlockSpec(memory_space=pl.ANY), vmem, vmem, vmem],
        out_specs=vmem,
        scratch_shapes=[
            pltpu.VMEM((snap_count, channels, samples), bf16),
            pltpu.VMEM((samples, 256), bf16),
            pltpu.VMEM((half, columns), f32),
            pltpu.VMEM((half, columns), f32),
            pltpu.VMEM((half, columns), f32),
            pltpu.VMEM((half, columns), f32),
            pltpu.VMEM((devices, blocks * modes, LANES), bf16),
            pltpu.VMEM((devices, blocks * modes, LANES), bf16),
            pltpu.VMEM((devices, 8, LANES), f32),
            pltpu.VMEM((devices, 8, LANES), f32),
            pltpu.VMEM((devices * 8, LANES), f32),
            pltpu.VMEM((devices, 8, LANES), f32),
            pltpu.VMEM((8, LANES), f32),
            pltpu.VMEM((devices * 8, LANES), f32),
            pltpu.VMEM((modes * modes, LANES), bf16),
            pltpu.VMEM((modes * modes, LANES), bf16),
            pltpu.VMEM((ranges_total, depths), f32),
            pltpu.VMEM((devices, ranges_total, depths), f32),
            pltpu.VMEM((ranges_total, depths), f32),
            pltpu.SemaphoreType.DMA,
        ]
        + [dma] * 10,
        compiler_params=pltpu.CompilerParams(
            collective_id=0, has_side_effects=True, vmem_limit_bytes=40 * 2**20
        ),
    )(freq_columns, snapshots, shapes, phases, masked)


def per_device(*args):
    snapshots, freq_bins, mode_shapes, _, _, source_modes, segment_owner = args
    devices = lax.axis_size("chan")
    blocks = segment_owner.shape[0]
    freqs = freq_bins.shape[0]
    modes, depths = source_modes.shape[1:]
    fits = (
        snapshots.shape[0] == 2
        and 2 * 2 * freqs == devices * LANES
        and 4 * freqs // devices == LANES
        and blocks * RPB == devices
        and blocks * modes * modes == devices * 8 * LANES
        and 2 * modes == LANES
        and depths == LANES
        and math.isqrt(snapshots.shape[2]) ** 2 == snapshots.shape[2]
    )
    return per_device_fused(*args) if fits else per_device_plain(*args)


def solution(mesh):
    return jax.shard_map(
        per_device,
        mesh=mesh,
        in_specs=(P("groups", "chan", None), P(), P(None, None, "chan"), P(), P(), P(), P()),
        out_specs=P(("groups", "chan"), None),
        check_vma=False,
    )
```

```python
import functools
import math

import jax
import jax.numpy as jnp
from jax import lax
from jax.experimental import pallas as pl
from jax.experimental.pallas import tpu as pltpu
from jax.sharding import PartitionSpec as P

F = 512
RPB = 4


range_start = 1.0
range_step = 0.01


def dft_table(freq_bins, samples):
    sample_ids = jnp.arange(samples, dtype=jnp.int32)
    residue = freq_bins[:, None] * sample_ids[None, :] % samples
    angles = residue.astype(jnp.float32) * (2.0 * jnp.pi / samples)
    return jnp.stack([jnp.cos(angles), -jnp.sin(angles)]).astype(jnp.bfloat16)


def surface_terms(
    proj_flat,
    gram_rounded,
    traces,
    waves,
    source_modes,
    mode_counts,
    segment_owner,
    ranges_per_block,
    freq_total,
):
    segs, modes, depths = source_modes.shape
    freqs = proj_flat.shape[0]
    snaps = proj_flat.shape[2]
    highest = lax.Precision.HIGHEST
    proj_four = proj_flat.reshape(freqs, 2, snaps, segs, modes)
    proj_real = proj_four[:, 0]
    proj_imag = proj_four[:, 1]
    upper = jnp.concatenate([proj_real, proj_imag], axis=-1)
    lower = jnp.concatenate([proj_imag, -proj_real], axis=-1)
    coupling = jnp.concatenate([upper, lower], axis=1)
    coupling = jnp.transpose(coupling, (2, 0, 1, 3)).astype(jnp.float32)
    zero_block = jnp.zeros_like(gram_rounded)
    gram_double = jnp.concatenate(
        [
            jnp.concatenate([gram_rounded, zero_block], axis=2),
            jnp.concatenate([zero_block, gram_rounded], axis=2),
        ],
        axis=1,
    ).astype(jnp.float32)
    active = (jnp.arange(modes, dtype=jnp.int32)[None, :] < mode_counts[:, None]).astype(
        jnp.float32
    )
    masked = jnp.transpose(source_modes * active[:, :, None], (0, 2, 1))
    mode_double = jnp.concatenate([masked, masked], axis=-1)
    wave_t = jnp.transpose(waves, (0, 2, 1))
    wave_double = jnp.concatenate([wave_t, wave_t], axis=-1)
    lanes = jnp.arange(2 * modes, dtype=jnp.int32) < modes
    seg_ids = jnp.arange(segs, dtype=jnp.int32)
    blocks = segment_owner.shape[0]

    def one_block(items):
        block_id, owner = items
        pick = (seg_ids == owner).astype(jnp.float32)
        wave_block = jnp.einsum("s,sfm->fm", pick, wave_double, precision=highest)
        mode_block = jnp.einsum("s,szm->zm", pick, mode_double, precision=highest)
        coupling_block = jnp.einsum("s,sfkm->fkm", pick, coupling, precision=highest).astype(
            jnp.bfloat16
        )
        gram_block = jnp.einsum("s,smn->mn", pick, gram_double, precision=highest).astype(
            jnp.bfloat16
        )
        range_ids = block_id * ranges_per_block + jnp.arange(ranges_per_block, dtype=jnp.int32)
        ranges = range_start + range_step * range_ids.astype(jnp.float32)
        phases = wave_block[:, None, :] * ranges[None, :, None]
        trig = jnp.where(lanes[None, None, :], jnp.cos(phases), jnp.sin(phases))
        amplitude = mode_block[None, None, :, :] / jnp.sqrt(phases)[:, :, None, :]
        cells = ranges_per_block * depths
        replica = (
            (amplitude * trig[:, :, None, :]).reshape(freqs, cells, 2 * modes).astype(jnp.bfloat16)
        )
        beams = jnp.einsum(
            "fkm,fcm->fkc", coupling_block, replica, preferred_element_type=jnp.float32
        )
        powers = jnp.sum(beams * beams, axis=1)
        mapped = jnp.einsum("fcm,mn->fcn", replica, gram_block, preferred_element_type=jnp.float32)
        weight_norm = jnp.sum(replica.astype(jnp.float32) * mapped, axis=-1)
        bartlett = powers / (snaps * traces[:, None] * weight_norm)
        return (jnp.sum(bartlett, axis=0) / freq_total).reshape(ranges_per_block, depths)

    block_ids = jnp.arange(blocks, dtype=jnp.int32)
    parts = lax.map(one_block, (block_ids, segment_owner))
    return parts.reshape(blocks * ranges_per_block, depths)


def per_device_plain(
    snapshots, freq_bins, mode_shapes, mode_counts, wavenumbers, source_modes, segment_owner
):
    devices_chan = lax.axis_size("chan")
    samples = snapshots.shape[2]
    segs = mode_shapes.shape[0]
    modes = mode_shapes.shape[1]
    local_freqs = F // devices_chan
    table_values = dft_table(freq_bins, samples)
    spectra = jnp.einsum(
        "cft,lht->cflh", table_values, snapshots, preferred_element_type=jnp.float32
    ).astype(jnp.bfloat16)
    moved = lax.all_to_all(spectra, "chan", split_axis=1, concat_axis=3, tiled=True)
    traces = jnp.sum(jnp.square(moved.astype(jnp.float32)), axis=(0, 2, 3))
    piece = lax.all_gather(mode_shapes, "chan", axis=2, tiled=True)
    flat_piece = piece.reshape(segs * modes, piece.shape[2])
    projections = jnp.einsum("cflh,kh->fclk", moved, flat_piece, preferred_element_type=jnp.float32)
    proj_rounded = projections.astype(jnp.bfloat16)
    local_gram = jnp.einsum(
        "smh,snh->smn", mode_shapes, mode_shapes, preferred_element_type=jnp.float32
    )
    gram = lax.psum(local_gram.reshape(segs, modes * modes), "chan")
    gram_rounded = gram.reshape(segs, modes, modes).astype(jnp.bfloat16)
    first_freq = lax.axis_index("chan") * local_freqs
    local_waves = lax.dynamic_slice_in_dim(wavenumbers, first_freq, local_freqs, 2)
    partial_surface = surface_terms(
        proj_rounded,
        gram_rounded,
        traces,
        local_waves,
        source_modes,
        mode_counts,
        segment_owner,
        RPB,
        F,
    )
    own_rows = partial_surface.shape[0] // devices_chan
    total_surface = lax.psum(partial_surface, "chan")
    highest_value = jnp.max(total_surface)
    own_surface = lax.dynamic_slice_in_dim(
        total_surface, lax.axis_index("chan") * own_rows, own_rows, 0
    )
    return own_surface / highest_value


LANES = 128
MESH = pl.DeviceIdType.MESH
HIGHEST = lax.Precision.HIGHEST


def sincos_small(x):
    y = x * x
    sine = x + x * y * (
        -1.6666667e-1 + y * (8.3333333e-3 + y * (-1.9841270e-4 + y * 2.7557319e-6))
    )
    cosine = 1.0 + y * (
        -0.5 + y * (4.1666667e-2 + y * (-1.3888889e-3 + y * (2.4801587e-5 - y * 2.7557319e-7)))
    )
    return sine, cosine


def turn(quadrant, sine, cosine):
    odd = (quadrant & 1) == 1
    c = jnp.where(odd, sine, cosine)
    s = jnp.where(odd, cosine, sine)
    return (
        jnp.where((quadrant & 2) != 0, -s, s),
        jnp.where(((quadrant + 1) & 2) != 0, -c, c),
    )


def sincos_bins(q, samples):
    quarter = samples // 4
    q = q & (samples - 1)
    quadrant = (q + quarter // 2) // quarter
    x = (q - quadrant * quarter).astype(jnp.float32) * (2.0 * math.pi / samples)
    return turn(quadrant, *sincos_small(x))


def sincos_wide(x):
    n = jnp.floor(x * (2.0 / math.pi) + 0.5)
    y = ((x - n * 1.5703125) - n * 4.837512969970703125e-4) - n * 7.54978995489188216e-8
    return turn(n.astype(jnp.int32), *sincos_small(y))


def fused_kernel(
    devices,
    freq_ref,
    snaps_hbm,
    modes_ref,
    counts_ref,
    waves_ref,
    modes_source_ref,
    owner_ref,
    out_ref,
    snaps,
    table,
    cos_a,
    sin_a,
    cos_b,
    sin_b,
    kept,
    core_send,
    core_recv,
    side_kept,
    side_send,
    side_recv,
    far_kept,
    far_send,
    far_recv,
    trace_send,
    trace_recv,
    gram_part,
    gram_recv,
    gram_own,
    gram_full,
    terms_a,
    terms_b,
    surf_own,
    surf_recv,
    total_ref,
    load_sem,
    core_ssem,
    core_rsem,
    side_ssem,
    side_rsem,
    far_ssem,
    far_rsem,
    trace_ssem,
    trace_rsem,
    gram_ssem,
    gram_rsem,
    full_ssem,
    full_rsem,
    surf_ssem,
    surf_rsem,
):
    me = lax.axis_index("chan")
    snap_count = 2
    samples = snaps_hbm.shape[1]
    channels = snaps_hbm.shape[0] // snap_count
    blocks = owner_ref.shape[0]
    modes, depths = modes_source_ref.shape[1:]
    columns = 2 * freq_ref.shape[0] * freq_ref.shape[1]
    core = me % 2
    side = (me // 2) % 2
    far = me // 4
    other_core = far * 4 + side * 2 + 1 - core
    other_side = far * 4 + (1 - side) * 2 + core
    width = table.shape[1]
    f32 = jnp.float32

    barrier = pltpu.get_barrier_semaphore()
    for step in range(1, devices):
        pl.semaphore_signal(
            barrier, inc=1, device_id={"chan": (me + step) % devices}, device_id_type=MESH
        )
    load = pltpu.make_async_copy(snaps_hbm, snaps, load_sem)
    load.start()

    def send(src, dst, ssem, rsem, peer):
        return pltpu.make_async_remote_copy(
            src_ref=src,
            dst_ref=dst,
            send_sem=ssem,
            recv_sem=rsem,
            device_id={"chan": peer},
            device_id_type=MESH,
        )

    owners = [owner_ref[block] for block in range(blocks)]
    shapes = jnp.concatenate([modes_ref[owner] for owner in owners], axis=0)
    inner = lax.dot_general(shapes, shapes, (((1,), (1,)), ((), ())), preferred_element_type=f32)
    low_half = lax.broadcasted_iota(jnp.int32, (modes, LANES), 1) < modes
    for pair in range(blocks // 2):
        base = pair * LANES
        gram_part[pair * modes : (pair + 1) * modes, :] = jnp.where(
            low_half,
            inner[base : base + modes, base : base + LANES],
            inner[base + modes : base + LANES, base : base + LANES],
        )
    pl.semaphore_wait(barrier, devices - 1)

    @pl.loop(1, devices)
    def _(step):
        peer = (me + step) % devices
        send(
            gram_part.at[pl.ds(pl.multiple_of(peer * 8, 8), 8), :],
            gram_recv.at[me],
            gram_ssem.at[peer],
            gram_rsem.at[me],
            peer,
        ).start()

    gram_recv[me] = gram_part[pl.ds(pl.multiple_of(me * 8, 8), 8), :]

    half = cos_a.shape[0]
    lane = lax.broadcasted_iota(jnp.int32, (1, LANES), 1)
    quarter = LANES // 4
    group = lane // quarter
    pieces = []
    for piece in range(columns // LANES):
        here = freq_ref[piece // 2 : piece // 2 + 1, :]
        shifts = (2 * quarter, 3 * quarter, 3 * quarter, 0) if piece % 2 else (0, quarter, quarter, 2 * quarter)
        turned = [pltpu.roll(here, n, 1) if n else here for n in shifts]
        pieces.append(
            jnp.where(
                group == 0,
                turned[0],
                jnp.where(group == 1, turned[1], jnp.where(group == 2, turned[2], turned[3])),
            )
        )
    freqs = jnp.concatenate(pieces, axis=1)
    column = lax.broadcasted_iota(jnp.int32, (half, columns), 1)
    row = lax.broadcasted_iota(jnp.int32, (half, columns), 0)
    part_size = columns // devices // 2
    shift = ((column // part_size) & 1) * (samples // 4)
    sin_v, cos_v = sincos_bins(freqs * (row * half) + shift, samples)
    sin_a[...] = sin_v
    cos_a[...] = cos_v
    sin_v, cos_v = sincos_bins(freqs * row, samples)
    sin_b[...] = sin_v
    cos_b[...] = cos_v

    @pl.loop(1, devices)
    def _(step):
        peer = (me + step) % devices
        send(
            gram_part.at[pl.ds(0, 8), :],
            gram_recv.at[peer],
            gram_ssem.at[peer],
            gram_rsem.at[peer],
            peer,
        ).wait_recv()

    gram_own[...] = jnp.sum(gram_recv[...], axis=0)
    own_rows = pl.ds(pl.multiple_of(me * 8, 8), 8)
    gram_full[own_rows, :] = gram_own[...]

    @pl.loop(1, devices)
    def _(step):
        peer = (me + step) % devices
        send(
            gram_own, gram_full.at[own_rows, :], full_ssem.at[peer], full_rsem.at[me], peer
        ).start()

    load.wait()
    per_chunk = width // (columns // devices)
    chunk_count = columns // width
    wide_low = lax.broadcasted_iota(jnp.int32, (blocks * modes, LANES), 1) < LANES // 2
    thin_low = wide_low[:8]

    def core_copy(chunk):
        return send(
            core_send.at[chunk], core_recv.at[chunk], core_ssem.at[chunk], core_rsem.at[chunk], other_core
        )

    def side_copy(chunk):
        return send(
            side_send.at[chunk], side_recv.at[chunk], side_ssem.at[chunk], side_rsem.at[chunk], other_side
        )

    def far_copy(chunk, slot):
        peer = chunk * 4 + side * 2 + core
        return send(far_send.at[chunk], far_recv.at[slot], far_ssem.at[chunk], far_rsem.at[slot], peer)

    def chunk_of(step):
        return (far + 1 + step) % chunk_count

    def make(step):
        chunk = chunk_of(step)
        cols = pl.ds(pl.multiple_of(chunk * width, width), width)
        cb = cos_b[:, cols]
        sb = sin_b[:, cols]

        @pl.loop(0, half, unroll=4)
        def _(a):
            ca = cos_a[pl.ds(a, 1), cols]
            sa = sin_a[pl.ds(a, 1), cols]
            table[pl.ds(pl.multiple_of(a * half, half), half), :] = (ca * cb - sa * sb).astype(
                jnp.bfloat16
            )

        parts = []
        sums = []
        both = jnp.dot(snaps[...], table[...], preferred_element_type=f32).astype(jnp.bfloat16)
        for snap in range(snap_count):
            spectra = both[snap * channels : (snap + 1) * channels]
            wide = spectra.astype(f32)
            sums.append(jnp.broadcast_to(jnp.sum(wide * wide, axis=0, keepdims=True), (8, width)))
            parts.append(jnp.dot(shapes, spectra, preferred_element_type=f32))
        for pair in range(per_chunk // 2):
            lanes = slice(pair * LANES, (pair + 1) * LANES)
            p0, p1 = parts[0][:, lanes], parts[1][:, lanes]
            t0, t1 = sums[0][:, lanes], sums[1][:, lanes]
            first = jnp.where(wide_low, p0, pltpu.roll(p1, LANES // 2, 1))
            second = jnp.where(wide_low, pltpu.roll(p0, LANES // 2, 1), p1)
            kept[chunk, pair] = jnp.where(core == 0, first, second)
            core_send[chunk, pair] = jnp.where(core == 0, second, first).astype(jnp.bfloat16)
            dest = chunk * per_chunk + 2 * pair
            trace_send[dest] = jnp.where(thin_low, t0, pltpu.roll(t1, LANES // 2, 1))[:1]
            trace_send[dest + 1] = jnp.where(thin_low, pltpu.roll(t0, LANES // 2, 1), t1)[:1]
        core_copy(chunk).start()
        for k in range(per_chunk):
            dest = chunk * per_chunk + k

            @pl.when(dest != me)
            def _():
                send(
                    trace_send.at[dest],
                    trace_recv.at[me],
                    trace_ssem.at[dest],
                    trace_rsem.at[me],
                    dest,
                ).start()

    def add_core(step):
        chunk = chunk_of(step)
        core_copy(chunk).wait_recv()
        side_kept[chunk] = kept[chunk, side] + core_recv[chunk, side].astype(f32)
        side_send[chunk] = (kept[chunk, 1 - side] + core_recv[chunk, 1 - side].astype(f32)).astype(
            jnp.bfloat16
        )
        side_copy(chunk).start()

    def add_side(step, keep=False):
        chunk = chunk_of(step)
        side_copy(chunk).wait_recv()
        total = side_kept[chunk] + side_recv[chunk].astype(f32)
        if keep:
            far_kept[...] = total
        else:
            far_send[chunk] = total.astype(jnp.bfloat16)
            far_copy(chunk, far).start()

    last = chunk_count - 1

    @pl.loop(0, chunk_count)
    def _(step):
        make(step)

        @pl.when(step >= 1)
        def _():
            add_core(step - 1)

        @pl.when(step >= 2)
        def _():
            add_side(step - 2)

    add_core(last)
    add_side(last - 1)
    trace_recv[me] = trace_send[me]

    @pl.loop(1, devices)
    def _(step):
        peer = (me + step) % devices
        send(
            gram_own,
            gram_full.at[pl.ds(pl.multiple_of(peer * 8, 8), 8), :],
            full_ssem.at[peer],
            full_rsem.at[peer],
            peer,
        ).wait_recv()

    gram = gram_full[...].astype(jnp.bfloat16).astype(f32)
    wide_lane = lax.broadcasted_iota(jnp.int32, (modes, LANES), 1)
    mode_ids = lax.broadcasted_iota(jnp.int32, (modes, depths), 0)
    sources = []
    waves_sin = []
    waves_cos = []
    norms = []
    for block in range(blocks):
        wave = waves_ref[owners[block], :, pl.ds(pl.multiple_of((me // 4) * LANES, LANES), LANES)]
        wave = jnp.where(wide_lane // quarter == me % 4, wave, 0.0)
        wave = wave + pltpu.roll(wave, quarter, 1)
        wave = wave + pltpu.roll(wave, 2 * quarter, 1)
        range_ids = block * RPB + wide_lane // quarter
        phases = wave * (range_start + range_step * range_ids.astype(f32))
        sine, cosine = sincos_wide(phases)
        scale = 1.0 / jnp.sqrt(phases)
        sine, cosine = sine * scale, cosine * scale
        waves_sin.append(sine)
        waves_cos.append(cosine)
        source = jnp.where(
            mode_ids < counts_ref[owners[block]], modes_source_ref[owners[block]], 0.0
        )
        sources.append(source)
        rows = slice((block // 2) * modes, (block // 2 + 1) * modes)
        for m in range(modes):
            lane = (block % 2) * modes + m
            at = slice(m * modes, (m + 1) * modes)
            terms_a[at, :] = (cosine[m : m + 1] * cosine + sine[m : m + 1] * sine).astype(
                jnp.bfloat16
            )
            terms_b[at, :] = (
                gram[rows, lane : lane + 1] * (source[m : m + 1] * source)
            ).astype(jnp.bfloat16)
        norms.append(
            lax.dot_general(
                terms_a[...],
                terms_b[...],
                (((0,), (0,)), ((), ())),
                preferred_element_type=f32,
            )
        )

    add_side(last, keep=True)

    @pl.loop(1, devices)
    def _(step):
        peer = (me + step) % devices
        send(
            trace_send.at[peer],
            trace_recv.at[peer],
            trace_ssem.at[peer],
            trace_rsem.at[peer],
            peer,
        ).wait_recv()

    proj = far_kept[...]
    for step in range(1, chunk_count):
        slot = (far + step) % chunk_count
        far_copy(slot, slot).wait_recv()
        proj = proj + far_recv[slot].astype(f32)
    proj = proj.astype(jnp.bfloat16)
    trace = jnp.broadcast_to(jnp.sum(trace_recv[...], axis=0), (8, LANES))
    trace = trace + pltpu.roll(trace, 2 * quarter, 1)
    trace = trace + pltpu.roll(trace, quarter, 1)
    level = (1.0 / jnp.sqrt(snap_count * trace))[:1]

    pick_in = lax.broadcasted_iota(jnp.int32, (LANES, 4 * LANES), 0)
    pick_out = lax.broadcasted_iota(jnp.int32, (LANES, 4 * LANES), 1)
    pick = (pick_in // quarter == pick_out // LANES) & (pick_in % quarter == pick_out % quarter)
    spread = jnp.dot(proj, pick.astype(f32).astype(jnp.bfloat16), preferred_element_type=f32)
    for block in range(blocks):
        sine, cosine = waves_sin[block] * level, waves_cos[block] * level
        rows = slice(block * modes, (block + 1) * modes)
        coupled = []
        for snap in range(snap_count):
            real = spread[rows, (2 * snap) * LANES : (2 * snap + 1) * LANES]
            imag = spread[rows, (2 * snap + 1) * LANES : (2 * snap + 2) * LANES]
            coupled.append(cosine * real + sine * imag)
            coupled.append(cosine * imag - sine * real)
        coupled = jnp.concatenate(coupled, axis=1)
        coupled_high = coupled.astype(jnp.bfloat16)
        coupled_low = (coupled - coupled_high.astype(f32)).astype(jnp.bfloat16)
        source = sources[block]
        source_high = source.astype(jnp.bfloat16)
        source_low = (source - source_high.astype(f32)).astype(jnp.bfloat16)
        beams = lax.dot_general(
            jnp.concatenate([coupled_high, coupled_low, coupled_high], axis=0),
            jnp.concatenate([source_high, source_high, source_low], axis=0),
            (((0,), (0,)), ((), ())),
            preferred_element_type=f32,
        )
        squares = beams * beams
        power = (
            squares[:LANES]
            + squares[LANES : 2 * LANES]
            + squares[2 * LANES : 3 * LANES]
            + squares[3 * LANES :]
        )
        ratio = power / norms[block]
        for j in range(4):
            surf_own[block * 4 + j : block * 4 + j + 1, :] = jnp.sum(
                ratio[j * quarter : (j + 1) * quarter], axis=0, keepdims=True
            )

    surf_recv[me] = surf_own[...]

    @pl.loop(1, devices)
    def _(step):
        peer = (me + step) % devices
        send(surf_own, surf_recv.at[me], surf_ssem.at[peer], surf_rsem.at[me], peer).start()

    @pl.loop(1, devices)
    def _(step):
        peer = (me + step) % devices
        send(surf_own, surf_recv.at[peer], surf_ssem.at[peer], surf_rsem.at[peer], peer).wait_recv()

    total = jnp.sum(surf_recv[...], axis=0) / (columns // 2)
    total_ref[...] = total
    out_ref[...] = total_ref[pl.ds(me, 1), :] / jnp.max(total)

    @pl.loop(1, devices)
    def _(step):
        peer = (me + step) % devices
        send(
            gram_part.at[pl.ds(pl.multiple_of(peer * 8, 8), 8), :],
            gram_recv.at[me],
            gram_ssem.at[peer],
            gram_rsem.at[me],
            peer,
        ).wait_send()
        send(
            gram_own, gram_full.at[own_rows, :], full_ssem.at[peer], full_rsem.at[me], peer
        ).wait_send()
        send(
            trace_send.at[peer], trace_recv.at[me], trace_ssem.at[peer], trace_rsem.at[me], peer
        ).wait_send()
        send(surf_own, surf_recv.at[me], surf_ssem.at[peer], surf_rsem.at[me], peer).wait_send()

    @pl.loop(0, chunk_count)
    def _(chunk):
        core_copy(chunk).wait_send()
        side_copy(chunk).wait_send()

        @pl.when(chunk != far)
        def _():
            far_copy(chunk, far).wait_send()


def per_device_fused(
    snapshots, freq_bins, mode_shapes, mode_counts, wavenumbers, source_modes, segment_owner
):
    devices = lax.axis_size("chan")
    snap_count, channels, samples = snapshots.shape
    segs, modes, depths = source_modes.shape
    blocks = segment_owner.shape[0]
    freqs = freq_bins.shape[0]
    columns = 2 * freqs
    half = math.isqrt(samples)
    rows = blocks * modes
    f32, bf16 = jnp.float32, jnp.bfloat16
    ranges_total = blocks * RPB
    dma = pltpu.SemaphoreType.DMA((devices,))
    vmem = pl.BlockSpec(memory_space=pltpu.VMEM)
    smem = pl.BlockSpec(memory_space=pltpu.SMEM)
    few = pltpu.SemaphoreType.DMA((devices // 4,))
    return pl.pallas_call(
        functools.partial(fused_kernel, devices),
        out_shape=jax.ShapeDtypeStruct((1, depths), f32),
        in_specs=[vmem, pl.BlockSpec(memory_space=pl.ANY), vmem, smem, vmem, vmem, smem],
        out_specs=vmem,
        scratch_shapes=[
            pltpu.VMEM((snap_count * channels, samples), bf16),
            pltpu.VMEM((samples, 256), bf16),
            pltpu.VMEM((half, columns), f32),
            pltpu.VMEM((half, columns), f32),
            pltpu.VMEM((half, columns), f32),
            pltpu.VMEM((half, columns), f32),
            pltpu.VMEM((devices // 4, 2, rows, LANES), f32),
            pltpu.VMEM((devices // 4, 2, rows, LANES), bf16),
            pltpu.VMEM((devices // 4, 2, rows, LANES), bf16),
            pltpu.VMEM((devices // 4, rows, LANES), f32),
            pltpu.VMEM((devices // 4, rows, LANES), bf16),
            pltpu.VMEM((devices // 4, rows, LANES), bf16),
            pltpu.VMEM((rows, LANES), f32),
            pltpu.VMEM((devices // 4, rows, LANES), bf16),
            pltpu.VMEM((devices // 4, rows, LANES), bf16),
            pltpu.VMEM((devices, 1, LANES), f32),
            pltpu.VMEM((devices, 1, LANES), f32),
            pltpu.VMEM((devices * 8, LANES), f32),
            pltpu.VMEM((devices, 8, LANES), f32),
            pltpu.VMEM((8, LANES), f32),
            pltpu.VMEM((devices * 8, LANES), f32),
            pltpu.VMEM((modes * modes, LANES), bf16),
            pltpu.VMEM((modes * modes, LANES), bf16),
            pltpu.VMEM((ranges_total, depths), f32),
            pltpu.VMEM((devices, ranges_total, depths), f32),
            pltpu.VMEM((ranges_total, depths), f32),
            pltpu.SemaphoreType.DMA,
        ]
        + [few] * 6
        + [dma] * 8,
        compiler_params=pltpu.CompilerParams(
            collective_id=0, has_side_effects=True, vmem_limit_bytes=40 * 2**20
        ),
    )(
        freq_bins.reshape(freqs // LANES, LANES),
        snapshots.reshape(snap_count * channels, samples),
        mode_shapes,
        mode_counts,
        wavenumbers,
        source_modes,
        segment_owner,
    )


def per_device(*args):
    snapshots, freq_bins, mode_shapes, _, _, source_modes, segment_owner = args
    devices = lax.axis_size("chan")
    blocks = segment_owner.shape[0]
    freqs = freq_bins.shape[0]
    modes, depths = source_modes.shape[1:]
    fits = (
        snapshots.shape[0] == 2
        and 2 * 2 * freqs == devices * LANES
        and 4 * freqs // devices == LANES
        and blocks * RPB == devices
        and blocks * modes * modes == devices * 8 * LANES
        and 2 * modes == LANES
        and depths == LANES
        and math.isqrt(snapshots.shape[2]) ** 2 == snapshots.shape[2]
    )
    return per_device_fused(*args) if fits else per_device_plain(*args)


def solution(mesh):
    return jax.shard_map(
        per_device,
        mesh=mesh,
        in_specs=(P("groups", "chan", None), P(), P(None, None, "chan"), P(), P(), P(), P()),
        out_specs=P(("groups", "chan"), None),
        check_vma=False,
    )
```

```python
import functools
import math

import jax
import jax.numpy as jnp
from jax import lax
from jax.experimental import pallas as pl
from jax.experimental.pallas import tpu as pltpu
from jax.sharding import PartitionSpec as P

F = 512
RPB = 4


range_start = 1.0
range_step = 0.01


def dft_table(freq_bins, samples):
    sample_ids = jnp.arange(samples, dtype=jnp.int32)
    residue = freq_bins[:, None] * sample_ids[None, :] % samples
    angles = residue.astype(jnp.float32) * (2.0 * jnp.pi / samples)
    return jnp.stack([jnp.cos(angles), -jnp.sin(angles)]).astype(jnp.bfloat16)


def surface_terms(
    proj_flat,
    gram_rounded,
    traces,
    waves,
    source_modes,
    mode_counts,
    segment_owner,
    ranges_per_block,
    freq_total,
):
    segs, modes, depths = source_modes.shape
    freqs = proj_flat.shape[0]
    snaps = proj_flat.shape[2]
    highest = lax.Precision.HIGHEST
    proj_four = proj_flat.reshape(freqs, 2, snaps, segs, modes)
    proj_real = proj_four[:, 0]
    proj_imag = proj_four[:, 1]
    upper = jnp.concatenate([proj_real, proj_imag], axis=-1)
    lower = jnp.concatenate([proj_imag, -proj_real], axis=-1)
    coupling = jnp.concatenate([upper, lower], axis=1)
    coupling = jnp.transpose(coupling, (2, 0, 1, 3)).astype(jnp.float32)
    zero_block = jnp.zeros_like(gram_rounded)
    gram_double = jnp.concatenate(
        [
            jnp.concatenate([gram_rounded, zero_block], axis=2),
            jnp.concatenate([zero_block, gram_rounded], axis=2),
        ],
        axis=1,
    ).astype(jnp.float32)
    active = (jnp.arange(modes, dtype=jnp.int32)[None, :] < mode_counts[:, None]).astype(
        jnp.float32
    )
    masked = jnp.transpose(source_modes * active[:, :, None], (0, 2, 1))
    mode_double = jnp.concatenate([masked, masked], axis=-1)
    wave_t = jnp.transpose(waves, (0, 2, 1))
    wave_double = jnp.concatenate([wave_t, wave_t], axis=-1)
    lanes = jnp.arange(2 * modes, dtype=jnp.int32) < modes
    seg_ids = jnp.arange(segs, dtype=jnp.int32)
    blocks = segment_owner.shape[0]

    def one_block(items):
        block_id, owner = items
        pick = (seg_ids == owner).astype(jnp.float32)
        wave_block = jnp.einsum("s,sfm->fm", pick, wave_double, precision=highest)
        mode_block = jnp.einsum("s,szm->zm", pick, mode_double, precision=highest)
        coupling_block = jnp.einsum("s,sfkm->fkm", pick, coupling, precision=highest).astype(
            jnp.bfloat16
        )
        gram_block = jnp.einsum("s,smn->mn", pick, gram_double, precision=highest).astype(
            jnp.bfloat16
        )
        range_ids = block_id * ranges_per_block + jnp.arange(ranges_per_block, dtype=jnp.int32)
        ranges = range_start + range_step * range_ids.astype(jnp.float32)
        phases = wave_block[:, None, :] * ranges[None, :, None]
        trig = jnp.where(lanes[None, None, :], jnp.cos(phases), jnp.sin(phases))
        amplitude = mode_block[None, None, :, :] / jnp.sqrt(phases)[:, :, None, :]
        cells = ranges_per_block * depths
        replica = (
            (amplitude * trig[:, :, None, :]).reshape(freqs, cells, 2 * modes).astype(jnp.bfloat16)
        )
        beams = jnp.einsum(
            "fkm,fcm->fkc", coupling_block, replica, preferred_element_type=jnp.float32
        )
        powers = jnp.sum(beams * beams, axis=1)
        mapped = jnp.einsum("fcm,mn->fcn", replica, gram_block, preferred_element_type=jnp.float32)
        weight_norm = jnp.sum(replica.astype(jnp.float32) * mapped, axis=-1)
        bartlett = powers / (snaps * traces[:, None] * weight_norm)
        return (jnp.sum(bartlett, axis=0) / freq_total).reshape(ranges_per_block, depths)

    block_ids = jnp.arange(blocks, dtype=jnp.int32)
    parts = lax.map(one_block, (block_ids, segment_owner))
    return parts.reshape(blocks * ranges_per_block, depths)


def per_device_plain(
    snapshots, freq_bins, mode_shapes, mode_counts, wavenumbers, source_modes, segment_owner
):
    devices_chan = lax.axis_size("chan")
    samples = snapshots.shape[2]
    segs = mode_shapes.shape[0]
    modes = mode_shapes.shape[1]
    local_freqs = F // devices_chan
    table_values = dft_table(freq_bins, samples)
    spectra = jnp.einsum(
        "cft,lht->cflh", table_values, snapshots, preferred_element_type=jnp.float32
    ).astype(jnp.bfloat16)
    moved = lax.all_to_all(spectra, "chan", split_axis=1, concat_axis=3, tiled=True)
    traces = jnp.sum(jnp.square(moved.astype(jnp.float32)), axis=(0, 2, 3))
    piece = lax.all_gather(mode_shapes, "chan", axis=2, tiled=True)
    flat_piece = piece.reshape(segs * modes, piece.shape[2])
    projections = jnp.einsum("cflh,kh->fclk", moved, flat_piece, preferred_element_type=jnp.float32)
    proj_rounded = projections.astype(jnp.bfloat16)
    local_gram = jnp.einsum(
        "smh,snh->smn", mode_shapes, mode_shapes, preferred_element_type=jnp.float32
    )
    gram = lax.psum(local_gram.reshape(segs, modes * modes), "chan")
    gram_rounded = gram.reshape(segs, modes, modes).astype(jnp.bfloat16)
    first_freq = lax.axis_index("chan") * local_freqs
    local_waves = lax.dynamic_slice_in_dim(wavenumbers, first_freq, local_freqs, 2)
    partial_surface = surface_terms(
        proj_rounded,
        gram_rounded,
        traces,
        local_waves,
        source_modes,
        mode_counts,
        segment_owner,
        RPB,
        F,
    )
    own_rows = partial_surface.shape[0] // devices_chan
    total_surface = lax.psum(partial_surface, "chan")
    highest_value = jnp.max(total_surface)
    own_surface = lax.dynamic_slice_in_dim(
        total_surface, lax.axis_index("chan") * own_rows, own_rows, 0
    )
    return own_surface / highest_value


LANES = 128
MESH = pl.DeviceIdType.MESH
HIGHEST = lax.Precision.HIGHEST


def sincos_small(x):
    y = x * x
    sine = x + x * y * (
        -1.6666667e-1 + y * (8.3333333e-3 + y * (-1.9841270e-4 + y * 2.7557319e-6))
    )
    cosine = 1.0 + y * (
        -0.5 + y * (4.1666667e-2 + y * (-1.3888889e-3 + y * (2.4801587e-5 - y * 2.7557319e-7)))
    )
    return sine, cosine


def turn(quadrant, sine, cosine):
    odd = (quadrant & 1) == 1
    c = jnp.where(odd, sine, cosine)
    s = jnp.where(odd, cosine, sine)
    return (
        jnp.where((quadrant & 2) != 0, -s, s),
        jnp.where(((quadrant + 1) & 2) != 0, -c, c),
    )


def sincos_bins(q, samples):
    quarter = samples // 4
    q = q & (samples - 1)
    quadrant = (q + quarter // 2) // quarter
    x = (q - quadrant * quarter).astype(jnp.float32) * (2.0 * math.pi / samples)
    return turn(quadrant, *sincos_small(x))


def sincos_wide(x):
    n = jnp.floor(x * (2.0 / math.pi) + 0.5)
    y = ((x - n * 1.5703125) - n * 4.837512969970703125e-4) - n * 7.54978995489188216e-8
    return turn(n.astype(jnp.int32), *sincos_small(y))


def fused_kernel(
    devices,
    freq_hbm,
    snaps_hbm,
    modes_hbm,
    counts_hbm,
    waves_hbm,
    source_hbm,
    owner_hbm,
    out_ref,
    freq_ref,
    modes_ref,
    counts_ref,
    waves_ref,
    modes_source_ref,
    owner_ref,
    snaps,
    table,
    cos_a,
    sin_a,
    cos_b,
    sin_b,
    kept,
    core_send,
    core_recv,
    side_kept,
    side_send,
    side_recv,
    far_kept,
    far_send,
    far_recv,
    trace_send,
    trace_recv,
    gram_part,
    gram_recv,
    gram_own,
    gram_full,
    terms_a,
    terms_b,
    surf_own,
    surf_recv,
    total_ref,
    load_sem,
    core_ssem,
    core_rsem,
    side_ssem,
    side_rsem,
    far_ssem,
    far_rsem,
    trace_ssem,
    trace_rsem,
    gram_ssem,
    gram_rsem,
    full_ssem,
    full_rsem,
    surf_ssem,
    surf_rsem,
):
    me = lax.axis_index("chan")
    snap_count = 2
    samples = snaps_hbm.shape[1]
    channels = snaps_hbm.shape[0] // snap_count
    blocks = owner_ref.shape[0]
    modes, depths = modes_source_ref.shape[1:]
    columns = 2 * freq_ref.shape[0] * freq_ref.shape[1]
    core = me % 2
    side = (me // 2) % 2
    far = me // 4
    other_core = far * 4 + side * 2 + 1 - core
    other_side = far * 4 + (1 - side) * 2 + core
    width = table.shape[1]
    f32 = jnp.float32

    barrier = pltpu.get_barrier_semaphore()
    for step in range(1, devices):
        pl.semaphore_signal(
            barrier, inc=1, device_id={"chan": (me + step) % devices}, device_id_type=MESH
        )
    window = pl.ds(pl.multiple_of((me // 4) * LANES, LANES), LANES)
    loads = [
        pltpu.make_async_copy(src, dst, load_sem.at[n])
        for n, (src, dst) in enumerate(
            [
                (freq_hbm, freq_ref),
                (owner_hbm, owner_ref),
                (counts_hbm, counts_ref),
                (modes_hbm, modes_ref),
                (source_hbm, modes_source_ref),
                (waves_hbm.at[:, :, window], waves_ref),
                (snaps_hbm, snaps),
            ]
        )
    ]
    for load in loads:
        load.start()

    def send(src, dst, ssem, rsem, peer):
        return pltpu.make_async_remote_copy(
            src_ref=src,
            dst_ref=dst,
            send_sem=ssem,
            recv_sem=rsem,
            device_id={"chan": peer},
            device_id_type=MESH,
        )

    half = cos_a.shape[0]
    loads[0].wait()
    lane = lax.broadcasted_iota(jnp.int32, (1, LANES), 1)
    quarter = LANES // 4
    group = lane // quarter
    pieces = []
    for piece in range(columns // LANES):
        here = freq_ref[piece // 2 : piece // 2 + 1, :]
        shifts = (2 * quarter, 3 * quarter, 3 * quarter, 0) if piece % 2 else (0, quarter, quarter, 2 * quarter)
        turned = [pltpu.roll(here, n, 1) if n else here for n in shifts]
        pieces.append(
            jnp.where(
                group == 0,
                turned[0],
                jnp.where(group == 1, turned[1], jnp.where(group == 2, turned[2], turned[3])),
            )
        )
    freqs = jnp.concatenate(pieces, axis=1)
    column = lax.broadcasted_iota(jnp.int32, (half, columns), 1)
    row = lax.broadcasted_iota(jnp.int32, (half, columns), 0)
    part_size = columns // devices // 2
    shift = ((column // part_size) & 1) * (samples // 4)
    sin_v, cos_v = sincos_bins(freqs * (row * half) + shift, samples)
    sin_a[...] = sin_v
    cos_a[...] = cos_v
    sin_v, cos_v = sincos_bins(freqs * row, samples)
    sin_b[...] = sin_v
    cos_b[...] = cos_v

    for load in loads[1:4]:
        load.wait()
    owners = [owner_ref[block] for block in range(blocks)]
    shapes = jnp.concatenate([modes_ref[owner] for owner in owners], axis=0)
    inner = lax.dot_general(shapes, shapes, (((1,), (1,)), ((), ())), preferred_element_type=f32)
    low_half = lax.broadcasted_iota(jnp.int32, (modes, LANES), 1) < modes
    for pair in range(blocks // 2):
        base = pair * LANES
        gram_part[pair * modes : (pair + 1) * modes, :] = jnp.where(
            low_half,
            inner[base : base + modes, base : base + LANES],
            inner[base + modes : base + LANES, base : base + LANES],
        )
    pl.semaphore_wait(barrier, devices - 1)

    @pl.loop(1, devices)
    def _(step):
        peer = (me + step) % devices
        send(
            gram_part.at[pl.ds(pl.multiple_of(peer * 8, 8), 8), :],
            gram_recv.at[me],
            gram_ssem.at[peer],
            gram_rsem.at[me],
            peer,
        ).start()

    gram_recv[me] = gram_part[pl.ds(pl.multiple_of(me * 8, 8), 8), :]

    for load in loads[4:]:
        load.wait()
    own_rows = pl.ds(pl.multiple_of(me * 8, 8), 8)
    per_chunk = width // (columns // devices)
    chunk_count = columns // width
    wide_low = lax.broadcasted_iota(jnp.int32, (blocks * modes, LANES), 1) < LANES // 2
    thin_low = wide_low[:8]

    def core_copy(chunk):
        return send(
            core_send.at[chunk], core_recv.at[chunk], core_ssem.at[chunk], core_rsem.at[chunk], other_core
        )

    def side_copy(chunk):
        return send(
            side_send.at[chunk], side_recv.at[chunk], side_ssem.at[chunk], side_rsem.at[chunk], other_side
        )

    def far_copy(chunk, slot):
        peer = chunk * 4 + side * 2 + core
        return send(far_send.at[chunk], far_recv.at[slot], far_ssem.at[chunk], far_rsem.at[slot], peer)

    def chunk_of(step):
        return (far + 1 + step) % chunk_count

    def make(step):
        chunk = chunk_of(step)
        cols = pl.ds(pl.multiple_of(chunk * width, width), width)
        cb = cos_b[:, cols]
        sb = sin_b[:, cols]

        def build(first):
            for a in range(first, first + half // 4):
                ca = cos_a[a : a + 1, cols]
                sa = sin_a[a : a + 1, cols]
                table[a * half : (a + 1) * half, :] = (ca * cb - sa * sb).astype(jnp.bfloat16)

        parts = []
        sums = []
        build(0)
        both = None
        for quart in range(4):
            rows = slice(quart * samples // 4, (quart + 1) * samples // 4)
            term = jnp.dot(snaps[:, rows], table[rows, :], preferred_element_type=f32)
            if quart < 3:
                build((quart + 1) * half // 4)
            both = term if both is None else both + term
        both = both.astype(jnp.bfloat16)
        for snap in range(snap_count):
            spectra = both[snap * channels : (snap + 1) * channels]
            wide = spectra.astype(f32)
            sums.append(jnp.broadcast_to(jnp.sum(wide * wide, axis=0, keepdims=True), (8, width)))
            parts.append(jnp.dot(shapes, spectra, preferred_element_type=f32))
        for pair in range(per_chunk // 2):
            lanes = slice(pair * LANES, (pair + 1) * LANES)
            p0, p1 = parts[0][:, lanes], parts[1][:, lanes]
            t0, t1 = sums[0][:, lanes], sums[1][:, lanes]
            first = jnp.where(wide_low, p0, pltpu.roll(p1, LANES // 2, 1))
            second = jnp.where(wide_low, pltpu.roll(p0, LANES // 2, 1), p1)
            kept[chunk, pair] = jnp.where(core == 0, first, second)
            core_send[chunk, pair] = jnp.where(core == 0, second, first).astype(jnp.bfloat16)
            dest = chunk * per_chunk + 2 * pair
            trace_send[dest] = jnp.where(thin_low, t0, pltpu.roll(t1, LANES // 2, 1))[:1]
            trace_send[dest + 1] = jnp.where(thin_low, pltpu.roll(t0, LANES // 2, 1), t1)[:1]
        core_copy(chunk).start()
        for k in range(per_chunk):
            dest = chunk * per_chunk + k

            @pl.when(dest != me)
            def _():
                send(
                    trace_send.at[dest],
                    trace_recv.at[me],
                    trace_ssem.at[dest],
                    trace_rsem.at[me],
                    dest,
                ).start()

    def add_core(step):
        chunk = chunk_of(step)
        core_copy(chunk).wait_recv()
        side_kept[chunk] = kept[chunk, side] + core_recv[chunk, side].astype(f32)
        side_send[chunk] = (kept[chunk, 1 - side] + core_recv[chunk, 1 - side].astype(f32)).astype(
            jnp.bfloat16
        )
        side_copy(chunk).start()

    def add_side(step, keep=False):
        chunk = chunk_of(step)
        side_copy(chunk).wait_recv()
        total = side_kept[chunk] + side_recv[chunk].astype(f32)
        if keep:
            far_kept[...] = total
        else:
            far_send[chunk] = total.astype(jnp.bfloat16)
            far_copy(chunk, far).start()

    def gram_share():
        @pl.loop(1, devices)
        def _(step):
            peer = (me + step) % devices
            send(
                gram_part.at[pl.ds(0, 8), :],
                gram_recv.at[peer],
                gram_ssem.at[peer],
                gram_rsem.at[peer],
                peer,
            ).wait_recv()

        gram_own[...] = jnp.sum(gram_recv[...], axis=0)
        gram_full[own_rows, :] = gram_own[...]

        @pl.loop(1, devices)
        def _(step):
            peer = (me + step) % devices
            send(
                gram_own, gram_full.at[own_rows, :], full_ssem.at[peer], full_rsem.at[me], peer
            ).start()

    last = chunk_count - 1

    @pl.loop(0, chunk_count)
    def _(step):
        make(step)

        @pl.when(step == 0)
        def _():
            gram_share()

        @pl.when(step >= 1)
        def _():
            add_core(step - 1)

        @pl.when(step >= 2)
        def _():
            add_side(step - 2)

    add_core(last)
    add_side(last - 1)
    trace_recv[me] = trace_send[me]

    @pl.loop(1, devices)
    def _(step):
        peer = (me + step) % devices
        send(
            gram_own,
            gram_full.at[pl.ds(pl.multiple_of(peer * 8, 8), 8), :],
            full_ssem.at[peer],
            full_rsem.at[peer],
            peer,
        ).wait_recv()

    gram = gram_full[...].astype(jnp.bfloat16).astype(f32)
    wide_lane = lax.broadcasted_iota(jnp.int32, (modes, LANES), 1)
    mode_ids = lax.broadcasted_iota(jnp.int32, (modes, depths), 0)
    sources = []
    waves_sin = []
    waves_cos = []
    norms = []
    for block in range(blocks):
        wave = waves_ref[owners[block]]
        wave = jnp.where(wide_lane // quarter == me % 4, wave, 0.0)
        wave = wave + pltpu.roll(wave, quarter, 1)
        wave = wave + pltpu.roll(wave, 2 * quarter, 1)
        range_ids = block * RPB + wide_lane // quarter
        phases = wave * (range_start + range_step * range_ids.astype(f32))
        sine, cosine = sincos_wide(phases)
        scale = 1.0 / jnp.sqrt(phases)
        sine, cosine = sine * scale, cosine * scale
        waves_sin.append(sine)
        waves_cos.append(cosine)
        source = jnp.where(
            mode_ids < counts_ref[owners[block]], modes_source_ref[owners[block]], 0.0
        )
        sources.append(source)
        rows = slice((block // 2) * modes, (block // 2 + 1) * modes)
        for m in range(modes):
            lane = (block % 2) * modes + m
            at = slice(m * modes, (m + 1) * modes)
            terms_a[at, :] = (cosine[m : m + 1] * cosine + sine[m : m + 1] * sine).astype(
                jnp.bfloat16
            )
            terms_b[at, :] = (
                gram[rows, lane : lane + 1] * (source[m : m + 1] * source)
            ).astype(jnp.bfloat16)
        norms.append(
            lax.dot_general(
                terms_a[...],
                terms_b[...],
                (((0,), (0,)), ((), ())),
                preferred_element_type=f32,
            )
        )

    add_side(last, keep=True)

    @pl.loop(1, devices)
    def _(step):
        peer = (me + step) % devices
        send(
            trace_send.at[peer],
            trace_recv.at[peer],
            trace_ssem.at[peer],
            trace_rsem.at[peer],
            peer,
        ).wait_recv()

    proj = far_kept[...]
    for step in range(1, chunk_count):
        slot = (far + step) % chunk_count
        far_copy(slot, slot).wait_recv()
        proj = proj + far_recv[slot].astype(f32)
    proj = proj.astype(jnp.bfloat16)
    trace = jnp.broadcast_to(jnp.sum(trace_recv[...], axis=0), (8, LANES))
    trace = trace + pltpu.roll(trace, 2 * quarter, 1)
    trace = trace + pltpu.roll(trace, quarter, 1)
    level = (1.0 / jnp.sqrt(snap_count * trace))[:1]

    pick_in = lax.broadcasted_iota(jnp.int32, (LANES, 4 * LANES), 0)
    pick_out = lax.broadcasted_iota(jnp.int32, (LANES, 4 * LANES), 1)
    pick = (pick_in // quarter == pick_out // LANES) & (pick_in % quarter == pick_out % quarter)
    spread = jnp.dot(proj, pick.astype(f32).astype(jnp.bfloat16), preferred_element_type=f32)
    for block in range(blocks):
        sine, cosine = waves_sin[block] * level, waves_cos[block] * level
        rows = slice(block * modes, (block + 1) * modes)
        coupled = []
        for snap in range(snap_count):
            real = spread[rows, (2 * snap) * LANES : (2 * snap + 1) * LANES]
            imag = spread[rows, (2 * snap + 1) * LANES : (2 * snap + 2) * LANES]
            coupled.append(cosine * real + sine * imag)
            coupled.append(cosine * imag - sine * real)
        coupled = jnp.concatenate(coupled, axis=1)
        coupled_high = coupled.astype(jnp.bfloat16)
        coupled_low = (coupled - coupled_high.astype(f32)).astype(jnp.bfloat16)
        source = sources[block]
        source_high = source.astype(jnp.bfloat16)
        source_low = (source - source_high.astype(f32)).astype(jnp.bfloat16)
        beams = lax.dot_general(
            jnp.concatenate([coupled_high, coupled_low, coupled_high], axis=0),
            jnp.concatenate([source_high, source_high, source_low], axis=0),
            (((0,), (0,)), ((), ())),
            preferred_element_type=f32,
        )
        squares = beams * beams
        power = (
            squares[:LANES]
            + squares[LANES : 2 * LANES]
            + squares[2 * LANES : 3 * LANES]
            + squares[3 * LANES :]
        )
        ratio = power / norms[block]
        for j in range(4):
            surf_own[block * 4 + j : block * 4 + j + 1, :] = jnp.sum(
                ratio[j * quarter : (j + 1) * quarter], axis=0, keepdims=True
            )

    surf_recv[me] = surf_own[...]

    @pl.loop(1, devices)
    def _(step):
        peer = (me + step) % devices
        send(surf_own, surf_recv.at[me], surf_ssem.at[peer], surf_rsem.at[me], peer).start()

    @pl.loop(1, devices)
    def _(step):
        peer = (me + step) % devices
        send(surf_own, surf_recv.at[peer], surf_ssem.at[peer], surf_rsem.at[peer], peer).wait_recv()

    total = jnp.sum(surf_recv[...], axis=0) / (columns // 2)
    total_ref[...] = total
    out_ref[...] = total_ref[pl.ds(me, 1), :] / jnp.max(total)

    @pl.loop(1, devices)
    def _(step):
        peer = (me + step) % devices
        send(
            gram_part.at[pl.ds(pl.multiple_of(peer * 8, 8), 8), :],
            gram_recv.at[me],
            gram_ssem.at[peer],
            gram_rsem.at[me],
            peer,
        ).wait_send()
        send(
            gram_own, gram_full.at[own_rows, :], full_ssem.at[peer], full_rsem.at[me], peer
        ).wait_send()
        send(
            trace_send.at[peer], trace_recv.at[me], trace_ssem.at[peer], trace_rsem.at[me], peer
        ).wait_send()
        send(surf_own, surf_recv.at[me], surf_ssem.at[peer], surf_rsem.at[me], peer).wait_send()

    @pl.loop(0, chunk_count)
    def _(chunk):
        core_copy(chunk).wait_send()
        side_copy(chunk).wait_send()

        @pl.when(chunk != far)
        def _():
            far_copy(chunk, far).wait_send()


def per_device_fused(
    snapshots, freq_bins, mode_shapes, mode_counts, wavenumbers, source_modes, segment_owner
):
    devices = lax.axis_size("chan")
    snap_count, channels, samples = snapshots.shape
    segs, modes, depths = source_modes.shape
    blocks = segment_owner.shape[0]
    freqs = freq_bins.shape[0]
    columns = 2 * freqs
    half = math.isqrt(samples)
    rows = blocks * modes
    f32, bf16 = jnp.float32, jnp.bfloat16
    ranges_total = blocks * RPB
    dma = pltpu.SemaphoreType.DMA((devices,))
    vmem = pl.BlockSpec(memory_space=pltpu.VMEM)
    few = pltpu.SemaphoreType.DMA((devices // 4,))
    return pl.pallas_call(
        functools.partial(fused_kernel, devices),
        out_shape=jax.ShapeDtypeStruct((1, depths), f32),
        in_specs=[pl.BlockSpec(memory_space=pltpu.HBM)] * 7,
        out_specs=vmem,
        scratch_shapes=[
            pltpu.VMEM((freqs // LANES, LANES), jnp.int32),
            pltpu.VMEM((segs, modes, channels), bf16),
            pltpu.SMEM((segs,), jnp.int32),
            pltpu.VMEM((segs, modes, LANES), f32),
            pltpu.VMEM((segs, modes, depths), f32),
            pltpu.SMEM((blocks,), jnp.int32),
            pltpu.VMEM((snap_count * channels, samples), bf16),
            pltpu.VMEM((samples, 256), bf16),
            pltpu.VMEM((half, columns), f32),
            pltpu.VMEM((half, columns), f32),
            pltpu.VMEM((half, columns), f32),
            pltpu.VMEM((half, columns), f32),
            pltpu.VMEM((devices // 4, 2, rows, LANES), f32),
            pltpu.VMEM((devices // 4, 2, rows, LANES), bf16),
            pltpu.VMEM((devices // 4, 2, rows, LANES), bf16),
            pltpu.VMEM((devices // 4, rows, LANES), f32),
            pltpu.VMEM((devices // 4, rows, LANES), bf16),
            pltpu.VMEM((devices // 4, rows, LANES), bf16),
            pltpu.VMEM((rows, LANES), f32),
            pltpu.VMEM((devices // 4, rows, LANES), bf16),
            pltpu.VMEM((devices // 4, rows, LANES), bf16),
            pltpu.VMEM((devices, 1, LANES), f32),
            pltpu.VMEM((devices, 1, LANES), f32),
            pltpu.VMEM((devices * 8, LANES), f32),
            pltpu.VMEM((devices, 8, LANES), f32),
            pltpu.VMEM((8, LANES), f32),
            pltpu.VMEM((devices * 8, LANES), f32),
            pltpu.VMEM((modes * modes, LANES), bf16),
            pltpu.VMEM((modes * modes, LANES), bf16),
            pltpu.VMEM((ranges_total, depths), f32),
            pltpu.VMEM((devices, ranges_total, depths), f32),
            pltpu.VMEM((ranges_total, depths), f32),
            pltpu.SemaphoreType.DMA((7,)),
        ]
        + [few] * 6
        + [dma] * 8,
        compiler_params=pltpu.CompilerParams(
            collective_id=0, has_side_effects=True, vmem_limit_bytes=62 * 2**20
        ),
    )(
        freq_bins.reshape(freqs // LANES, LANES),
        snapshots.reshape(snap_count * channels, samples),
        mode_shapes,
        mode_counts,
        wavenumbers,
        source_modes,
        segment_owner,
    )


def per_device(*args):
    snapshots, freq_bins, mode_shapes, _, _, source_modes, segment_owner = args
    devices = lax.axis_size("chan")
    blocks = segment_owner.shape[0]
    freqs = freq_bins.shape[0]
    modes, depths = source_modes.shape[1:]
    fits = (
        snapshots.shape[0] == 2
        and 2 * 2 * freqs == devices * LANES
        and 4 * freqs // devices == LANES
        and blocks * RPB == devices
        and blocks * modes * modes == devices * 8 * LANES
        and 2 * modes == LANES
        and depths == LANES
        and math.isqrt(snapshots.shape[2]) ** 2 == snapshots.shape[2]
    )
    return per_device_fused(*args) if fits else per_device_plain(*args)


def solution(mesh):
    return jax.shard_map(
        per_device,
        mesh=mesh,
        in_specs=(P("groups", "chan", None), P(), P(None, None, "chan"), P(), P(), P(), P()),
        out_specs=P(("groups", "chan"), None),
        check_vma=False,
    )
```

```python
import functools
import math

import jax
import jax.numpy as jnp
from jax import lax
from jax.experimental import pallas as pl
from jax.experimental.pallas import tpu as pltpu
from jax.sharding import PartitionSpec as P

F = 512
RPB = 4


range_start = 1.0
range_step = 0.01


def dft_table(freq_bins, samples):
    sample_ids = jnp.arange(samples, dtype=jnp.int32)
    residue = freq_bins[:, None] * sample_ids[None, :] % samples
    angles = residue.astype(jnp.float32) * (2.0 * jnp.pi / samples)
    return jnp.stack([jnp.cos(angles), -jnp.sin(angles)]).astype(jnp.bfloat16)


def surface_terms(
    proj_flat,
    gram_rounded,
    traces,
    waves,
    source_modes,
    mode_counts,
    segment_owner,
    ranges_per_block,
    freq_total,
):
    segs, modes, depths = source_modes.shape
    freqs = proj_flat.shape[0]
    snaps = proj_flat.shape[2]
    highest = lax.Precision.HIGHEST
    proj_four = proj_flat.reshape(freqs, 2, snaps, segs, modes)
    proj_real = proj_four[:, 0]
    proj_imag = proj_four[:, 1]
    upper = jnp.concatenate([proj_real, proj_imag], axis=-1)
    lower = jnp.concatenate([proj_imag, -proj_real], axis=-1)
    coupling = jnp.concatenate([upper, lower], axis=1)
    coupling = jnp.transpose(coupling, (2, 0, 1, 3)).astype(jnp.float32)
    zero_block = jnp.zeros_like(gram_rounded)
    gram_double = jnp.concatenate(
        [
            jnp.concatenate([gram_rounded, zero_block], axis=2),
            jnp.concatenate([zero_block, gram_rounded], axis=2),
        ],
        axis=1,
    ).astype(jnp.float32)
    active = (jnp.arange(modes, dtype=jnp.int32)[None, :] < mode_counts[:, None]).astype(
        jnp.float32
    )
    masked = jnp.transpose(source_modes * active[:, :, None], (0, 2, 1))
    mode_double = jnp.concatenate([masked, masked], axis=-1)
    wave_t = jnp.transpose(waves, (0, 2, 1))
    wave_double = jnp.concatenate([wave_t, wave_t], axis=-1)
    lanes = jnp.arange(2 * modes, dtype=jnp.int32) < modes
    seg_ids = jnp.arange(segs, dtype=jnp.int32)
    blocks = segment_owner.shape[0]

    def one_block(items):
        block_id, owner = items
        pick = (seg_ids == owner).astype(jnp.float32)
        wave_block = jnp.einsum("s,sfm->fm", pick, wave_double, precision=highest)
        mode_block = jnp.einsum("s,szm->zm", pick, mode_double, precision=highest)
        coupling_block = jnp.einsum("s,sfkm->fkm", pick, coupling, precision=highest).astype(
            jnp.bfloat16
        )
        gram_block = jnp.einsum("s,smn->mn", pick, gram_double, precision=highest).astype(
            jnp.bfloat16
        )
        range_ids = block_id * ranges_per_block + jnp.arange(ranges_per_block, dtype=jnp.int32)
        ranges = range_start + range_step * range_ids.astype(jnp.float32)
        phases = wave_block[:, None, :] * ranges[None, :, None]
        trig = jnp.where(lanes[None, None, :], jnp.cos(phases), jnp.sin(phases))
        amplitude = mode_block[None, None, :, :] / jnp.sqrt(phases)[:, :, None, :]
        cells = ranges_per_block * depths
        replica = (
            (amplitude * trig[:, :, None, :]).reshape(freqs, cells, 2 * modes).astype(jnp.bfloat16)
        )
        beams = jnp.einsum(
            "fkm,fcm->fkc", coupling_block, replica, preferred_element_type=jnp.float32
        )
        powers = jnp.sum(beams * beams, axis=1)
        mapped = jnp.einsum("fcm,mn->fcn", replica, gram_block, preferred_element_type=jnp.float32)
        weight_norm = jnp.sum(replica.astype(jnp.float32) * mapped, axis=-1)
        bartlett = powers / (snaps * traces[:, None] * weight_norm)
        return (jnp.sum(bartlett, axis=0) / freq_total).reshape(ranges_per_block, depths)

    block_ids = jnp.arange(blocks, dtype=jnp.int32)
    parts = lax.map(one_block, (block_ids, segment_owner))
    return parts.reshape(blocks * ranges_per_block, depths)


def per_device_plain(
    snapshots, freq_bins, mode_shapes, mode_counts, wavenumbers, source_modes, segment_owner
):
    devices_chan = lax.axis_size("chan")
    samples = snapshots.shape[2]
    segs = mode_shapes.shape[0]
    modes = mode_shapes.shape[1]
    local_freqs = F // devices_chan
    table_values = dft_table(freq_bins, samples)
    spectra = jnp.einsum(
        "cft,lht->cflh", table_values, snapshots, preferred_element_type=jnp.float32
    ).astype(jnp.bfloat16)
    moved = lax.all_to_all(spectra, "chan", split_axis=1, concat_axis=3, tiled=True)
    traces = jnp.sum(jnp.square(moved.astype(jnp.float32)), axis=(0, 2, 3))
    piece = lax.all_gather(mode_shapes, "chan", axis=2, tiled=True)
    flat_piece = piece.reshape(segs * modes, piece.shape[2])
    projections = jnp.einsum("cflh,kh->fclk", moved, flat_piece, preferred_element_type=jnp.float32)
    proj_rounded = projections.astype(jnp.bfloat16)
    local_gram = jnp.einsum(
        "smh,snh->smn", mode_shapes, mode_shapes, preferred_element_type=jnp.float32
    )
    gram = lax.psum(local_gram.reshape(segs, modes * modes), "chan")
    gram_rounded = gram.reshape(segs, modes, modes).astype(jnp.bfloat16)
    first_freq = lax.axis_index("chan") * local_freqs
    local_waves = lax.dynamic_slice_in_dim(wavenumbers, first_freq, local_freqs, 2)
    partial_surface = surface_terms(
        proj_rounded,
        gram_rounded,
        traces,
        local_waves,
        source_modes,
        mode_counts,
        segment_owner,
        RPB,
        F,
    )
    own_rows = partial_surface.shape[0] // devices_chan
    total_surface = lax.psum(partial_surface, "chan")
    highest_value = jnp.max(total_surface)
    own_surface = lax.dynamic_slice_in_dim(
        total_surface, lax.axis_index("chan") * own_rows, own_rows, 0
    )
    return own_surface / highest_value


LANES = 128
MESH = pl.DeviceIdType.MESH
HIGHEST = lax.Precision.HIGHEST


def sincos_small(x):
    y = x * x
    sine = x + x * y * (
        -1.6666667e-1 + y * (8.3333333e-3 + y * (-1.9841270e-4 + y * 2.7557319e-6))
    )
    cosine = 1.0 + y * (
        -0.5 + y * (4.1666667e-2 + y * (-1.3888889e-3 + y * (2.4801587e-5 - y * 2.7557319e-7)))
    )
    return sine, cosine


def turn(quadrant, sine, cosine):
    odd = (quadrant & 1) == 1
    c = jnp.where(odd, sine, cosine)
    s = jnp.where(odd, cosine, sine)
    return (
        jnp.where((quadrant & 2) != 0, -s, s),
        jnp.where(((quadrant + 1) & 2) != 0, -c, c),
    )


def sincos_bins(q, samples):
    quarter = samples // 4
    q = q & (samples - 1)
    quadrant = (q + quarter // 2) // quarter
    x = (q - quadrant * quarter).astype(jnp.float32) * (2.0 * math.pi / samples)
    return turn(quadrant, *sincos_small(x))


def sincos_wide(x):
    n = jnp.floor(x * (2.0 / math.pi) + 0.5)
    y = ((x - n * 1.5703125) - n * 4.837512969970703125e-4) - n * 7.54978995489188216e-8
    return turn(n.astype(jnp.int32), *sincos_small(y))


def fused_kernel(
    devices,
    freq_hbm,
    snaps_hbm,
    modes_hbm,
    counts_hbm,
    waves_hbm,
    source_hbm,
    owner_hbm,
    out_ref,
    freq_ref,
    modes_ref,
    counts_ref,
    waves_ref,
    modes_source_ref,
    owner_ref,
    snaps,
    table,
    cos_a,
    sin_a,
    cos_b,
    sin_b,
    kept,
    core_send,
    core_recv,
    side_kept,
    side_send,
    side_recv,
    far_kept,
    far_send,
    far_recv,
    trace_send,
    trace_recv,
    gram_part,
    gram_recv,
    gram_own,
    gram_full,
    terms_a,
    terms_b,
    surf_own,
    surf_recv,
    total_ref,
    load_sem,
    core_ssem,
    core_rsem,
    side_ssem,
    side_rsem,
    far_ssem,
    far_rsem,
    trace_ssem,
    trace_rsem,
    gram_ssem,
    gram_rsem,
    full_ssem,
    full_rsem,
    surf_ssem,
    surf_rsem,
):
    me = lax.axis_index("chan")
    snap_count = 2
    samples = snaps_hbm.shape[1]
    channels = snaps_hbm.shape[0] // snap_count
    blocks = owner_ref.shape[0]
    modes, depths = modes_source_ref.shape[1:]
    columns = 2 * freq_ref.shape[0] * freq_ref.shape[1]
    core = me % 2
    side = (me // 2) % 2
    far = me // 4
    other_core = far * 4 + side * 2 + 1 - core
    other_side = far * 4 + (1 - side) * 2 + core
    width = table.shape[1]
    f32 = jnp.float32

    barrier = pltpu.get_barrier_semaphore()
    for step in range(1, devices):
        pl.semaphore_signal(
            barrier, inc=1, device_id={"chan": (me + step) % devices}, device_id_type=MESH
        )
    window = pl.ds(pl.multiple_of((me // 4) * LANES, LANES), LANES)
    loads = [
        pltpu.make_async_copy(src, dst, load_sem.at[n])
        for n, (src, dst) in enumerate(
            [
                (freq_hbm, freq_ref),
                (owner_hbm, owner_ref),
                (counts_hbm, counts_ref),
                (modes_hbm, modes_ref),
                (source_hbm, modes_source_ref),
                (waves_hbm.at[:, :, window], waves_ref),
                (snaps_hbm, snaps),
            ]
        )
    ]
    for load in loads:
        load.start()

    def send(src, dst, ssem, rsem, peer):
        return pltpu.make_async_remote_copy(
            src_ref=src,
            dst_ref=dst,
            send_sem=ssem,
            recv_sem=rsem,
            device_id={"chan": peer},
            device_id_type=MESH,
        )

    half = cos_a.shape[0]
    loads[0].wait()
    lane = lax.broadcasted_iota(jnp.int32, (1, LANES), 1)
    quarter = LANES // 4
    group = lane // quarter
    pieces = []
    for piece in range(columns // LANES):
        here = freq_ref[piece // 2 : piece // 2 + 1, :]
        shifts = (2 * quarter, 3 * quarter, 3 * quarter, 0) if piece % 2 else (0, quarter, quarter, 2 * quarter)
        turned = [pltpu.roll(here, n, 1) if n else here for n in shifts]
        pieces.append(
            jnp.where(
                group == 0,
                turned[0],
                jnp.where(group == 1, turned[1], jnp.where(group == 2, turned[2], turned[3])),
            )
        )
    freqs = jnp.concatenate(pieces, axis=1)
    column = lax.broadcasted_iota(jnp.int32, (half, columns), 1)
    row = lax.broadcasted_iota(jnp.int32, (half, columns), 0)
    part_size = columns // devices // 2
    shift = ((column // part_size) & 1) * (samples // 4)
    sin_v, cos_v = sincos_bins(freqs * (row * half) + shift, samples)
    sin_a[...] = sin_v
    cos_a[...] = cos_v
    sin_v, cos_v = sincos_bins(freqs * row, samples)
    sin_b[...] = sin_v
    cos_b[...] = cos_v

    for load in loads[1:4]:
        load.wait()
    owners = [owner_ref[block] for block in range(blocks)]
    shapes = jnp.concatenate([modes_ref[owner] for owner in owners], axis=0)
    inner = lax.dot_general(shapes, shapes, (((1,), (1,)), ((), ())), preferred_element_type=f32)
    low_half = lax.broadcasted_iota(jnp.int32, (modes, LANES), 1) < modes
    for pair in range(blocks // 2):
        base = pair * LANES
        gram_part[pair * modes : (pair + 1) * modes, :] = jnp.where(
            low_half,
            inner[base : base + modes, base : base + LANES],
            inner[base + modes : base + LANES, base : base + LANES],
        )
    pl.semaphore_wait(barrier, devices - 1)

    @pl.loop(1, devices)
    def _(step):
        peer = (me + step) % devices
        send(
            gram_part.at[pl.ds(pl.multiple_of(peer * 8, 8), 8), :],
            gram_recv.at[me],
            gram_ssem.at[peer],
            gram_rsem.at[me],
            peer,
        ).start()

    gram_recv[me] = gram_part[pl.ds(pl.multiple_of(me * 8, 8), 8), :]

    for load in loads[4:]:
        load.wait()
    own_rows = pl.ds(pl.multiple_of(me * 8, 8), 8)
    per_chunk = width // (columns // devices)
    chunk_count = columns // width
    wide_low = lax.broadcasted_iota(jnp.int32, (blocks * modes, LANES), 1) < LANES // 2
    thin_low = wide_low[:8]

    def core_copy(chunk):
        return send(
            core_send.at[chunk], core_recv.at[chunk], core_ssem.at[chunk], core_rsem.at[chunk], other_core
        )

    def side_copy(chunk):
        return send(
            side_send.at[chunk], side_recv.at[chunk], side_ssem.at[chunk], side_rsem.at[chunk], other_side
        )

    def far_copy(chunk, slot):
        peer = chunk * 4 + side * 2 + core
        return send(far_send.at[chunk], far_recv.at[slot], far_ssem.at[chunk], far_rsem.at[slot], peer)

    def chunk_of(step):
        return (far + 1 + step) % chunk_count

    def make(step):
        chunk = chunk_of(step)
        cols = pl.ds(pl.multiple_of(chunk * width, width), width)
        cb = cos_b[:, cols]
        sb = sin_b[:, cols]

        def build(first):
            for a in range(first, first + half // 4):
                ca = cos_a[a : a + 1, cols]
                sa = sin_a[a : a + 1, cols]
                table[a * half : (a + 1) * half, :] = (ca * cb - sa * sb).astype(jnp.bfloat16)

        parts = []
        sums = []
        build(0)
        both = None
        for quart in range(4):
            rows = slice(quart * samples // 4, (quart + 1) * samples // 4)
            term = jnp.dot(snaps[:, rows], table[rows, :], preferred_element_type=f32)
            if quart < 3:
                build((quart + 1) * half // 4)
            both = term if both is None else both + term
        both = both.astype(jnp.bfloat16)
        for snap in range(snap_count):
            spectra = both[snap * channels : (snap + 1) * channels]
            wide = spectra.astype(f32)
            sums.append(jnp.broadcast_to(jnp.sum(wide * wide, axis=0, keepdims=True), (8, width)))
            parts.append(jnp.dot(shapes, spectra, preferred_element_type=f32))
        for pair in range(per_chunk // 2):
            lanes = slice(pair * LANES, (pair + 1) * LANES)
            p0, p1 = parts[0][:, lanes], parts[1][:, lanes]
            t0, t1 = sums[0][:, lanes], sums[1][:, lanes]
            first = jnp.where(wide_low, p0, pltpu.roll(p1, LANES // 2, 1))
            second = jnp.where(wide_low, pltpu.roll(p0, LANES // 2, 1), p1)
            kept[chunk, pair] = jnp.where(core == 0, first, second)
            core_send[chunk, pair] = jnp.where(core == 0, second, first).astype(jnp.bfloat16)
            dest = chunk * per_chunk + 2 * pair
            trace_send[dest] = jnp.where(thin_low, t0, pltpu.roll(t1, LANES // 2, 1))[:1]
            trace_send[dest + 1] = jnp.where(thin_low, pltpu.roll(t0, LANES // 2, 1), t1)[:1]
        core_copy(chunk).start()
        for k in range(per_chunk):
            dest = chunk * per_chunk + k

            @pl.when(dest != me)
            def _():
                send(
                    trace_send.at[dest],
                    trace_recv.at[me],
                    trace_ssem.at[dest],
                    trace_rsem.at[me],
                    dest,
                ).start()

    def add_core(step):
        chunk = chunk_of(step)
        core_copy(chunk).wait_recv()
        side_kept[chunk] = kept[chunk, side] + core_recv[chunk, side].astype(f32)
        side_send[chunk] = (kept[chunk, 1 - side] + core_recv[chunk, 1 - side].astype(f32)).astype(
            jnp.bfloat16
        )
        side_copy(chunk).start()

    def add_side(step, keep=False):
        chunk = chunk_of(step)
        side_copy(chunk).wait_recv()
        total = side_kept[chunk] + side_recv[chunk].astype(f32)
        if keep:
            far_kept[...] = total
        else:
            far_send[chunk] = total.astype(jnp.bfloat16)
            far_copy(chunk, far).start()

    def gram_share():
        @pl.loop(1, devices)
        def _(step):
            peer = (me + step) % devices
            send(
                gram_part.at[pl.ds(0, 8), :],
                gram_recv.at[peer],
                gram_ssem.at[peer],
                gram_rsem.at[peer],
                peer,
            ).wait_recv()

        gram_own[...] = jnp.sum(gram_recv[...], axis=0)
        gram_full[own_rows, :] = gram_own[...]

        @pl.loop(1, devices)
        def _(step):
            peer = (me + step) % devices
            send(
                gram_own, gram_full.at[own_rows, :], full_ssem.at[peer], full_rsem.at[me], peer
            ).start()

    last = chunk_count - 1

    @pl.loop(0, chunk_count)
    def _(step):
        make(step)

        @pl.when(step == 0)
        def _():
            gram_share()

        @pl.when(step >= 1)
        def _():
            add_core(step - 1)

        @pl.when(step >= 2)
        def _():
            add_side(step - 2)

    add_core(last)
    add_side(last - 1)
    trace_recv[me] = trace_send[me]

    @pl.loop(1, devices)
    def _(step):
        peer = (me + step) % devices
        send(
            gram_own,
            gram_full.at[pl.ds(pl.multiple_of(peer * 8, 8), 8), :],
            full_ssem.at[peer],
            full_rsem.at[peer],
            peer,
        ).wait_recv()

    gram = gram_full[...].astype(jnp.bfloat16).astype(f32)
    tile = 16
    first_tile = (lax.broadcasted_iota(jnp.int32, gram.shape, 0) % modes) // tile
    second_tile = (lax.broadcasted_iota(jnp.int32, gram.shape, 1) % modes) // tile
    gram = jnp.where(first_tile > second_tile, 2.0 * gram, gram)
    pairs = sum(tile * (modes - start) for start in range(0, modes, tile))
    wide_lane = lax.broadcasted_iota(jnp.int32, (modes, LANES), 1)
    mode_ids = lax.broadcasted_iota(jnp.int32, (modes, depths), 0)
    sources = []
    waves_sin = []
    waves_cos = []
    norms = []
    for block in range(blocks):
        wave = waves_ref[owners[block]]
        wave = jnp.where(wide_lane // quarter == me % 4, wave, 0.0)
        wave = wave + pltpu.roll(wave, quarter, 1)
        wave = wave + pltpu.roll(wave, 2 * quarter, 1)
        range_ids = block * RPB + wide_lane // quarter
        phases = wave * (range_start + range_step * range_ids.astype(f32))
        sine, cosine = sincos_wide(phases)
        scale = 1.0 / jnp.sqrt(phases)
        sine, cosine = sine * scale, cosine * scale
        waves_sin.append(sine)
        waves_cos.append(cosine)
        source = jnp.where(
            mode_ids < counts_ref[owners[block]], modes_source_ref[owners[block]], 0.0
        )
        sources.append(source)
        base = (block // 2) * modes
        filled = 0
        for m in range(modes):
            low = m // tile * tile
            lane = (block % 2) * modes + m
            at = slice(filled, filled + modes - low)
            filled += modes - low
            terms_a[at, :] = (
                cosine[m : m + 1] * cosine[low:] + sine[m : m + 1] * sine[low:]
            ).astype(jnp.bfloat16)
            terms_b[at, :] = (
                gram[base + low : base + modes, lane : lane + 1] * (source[m : m + 1] * source[low:])
            ).astype(jnp.bfloat16)
        norms.append(
            lax.dot_general(
                terms_a[:pairs],
                terms_b[:pairs],
                (((0,), (0,)), ((), ())),
                preferred_element_type=f32,
            )
        )

    add_side(last, keep=True)

    @pl.loop(1, devices)
    def _(step):
        peer = (me + step) % devices
        send(
            trace_send.at[peer],
            trace_recv.at[peer],
            trace_ssem.at[peer],
            trace_rsem.at[peer],
            peer,
        ).wait_recv()

    proj = far_kept[...]
    for step in range(1, chunk_count):
        slot = (far + step) % chunk_count
        far_copy(slot, slot).wait_recv()
        proj = proj + far_recv[slot].astype(f32)
    proj = proj.astype(jnp.bfloat16)
    trace = jnp.broadcast_to(jnp.sum(trace_recv[...], axis=0), (8, LANES))
    trace = trace + pltpu.roll(trace, 2 * quarter, 1)
    trace = trace + pltpu.roll(trace, quarter, 1)
    level = (1.0 / jnp.sqrt(snap_count * trace))[:1]

    pick_in = lax.broadcasted_iota(jnp.int32, (LANES, 4 * LANES), 0)
    pick_out = lax.broadcasted_iota(jnp.int32, (LANES, 4 * LANES), 1)
    pick = (pick_in // quarter == pick_out // LANES) & (pick_in % quarter == pick_out % quarter)
    spread = jnp.dot(proj, pick.astype(f32).astype(jnp.bfloat16), preferred_element_type=f32)
    for block in range(blocks):
        sine, cosine = waves_sin[block] * level, waves_cos[block] * level
        rows = slice(block * modes, (block + 1) * modes)
        coupled = []
        for snap in range(snap_count):
            real = spread[rows, (2 * snap) * LANES : (2 * snap + 1) * LANES]
            imag = spread[rows, (2 * snap + 1) * LANES : (2 * snap + 2) * LANES]
            coupled.append(cosine * real + sine * imag)
            coupled.append(cosine * imag - sine * real)
        coupled = jnp.concatenate(coupled, axis=1)
        coupled_high = coupled.astype(jnp.bfloat16)
        coupled_low = (coupled - coupled_high.astype(f32)).astype(jnp.bfloat16)
        source = sources[block]
        source_high = source.astype(jnp.bfloat16)
        source_low = (source - source_high.astype(f32)).astype(jnp.bfloat16)
        beams = lax.dot_general(
            jnp.concatenate([coupled_high, coupled_low, coupled_high], axis=0),
            jnp.concatenate([source_high, source_high, source_low], axis=0),
            (((0,), (0,)), ((), ())),
            preferred_element_type=f32,
        )
        squares = beams * beams
        power = (
            squares[:LANES]
            + squares[LANES : 2 * LANES]
            + squares[2 * LANES : 3 * LANES]
            + squares[3 * LANES :]
        )
        ratio = power / norms[block]
        for j in range(4):
            surf_own[block * 4 + j : block * 4 + j + 1, :] = jnp.sum(
                ratio[j * quarter : (j + 1) * quarter], axis=0, keepdims=True
            )

    near = me % 4

    def near_copy(step, slot):
        peer = (near + step) % 4
        return send(
            surf_own, surf_recv.at[slot], surf_ssem.at[peer], surf_rsem.at[slot], far * 4 + peer
        )

    def wide_copy(step, slot):
        peer = (far + step) % chunk_count
        return send(
            surf_recv.at[4 + far],
            surf_recv.at[4 + slot],
            surf_ssem.at[4 + peer],
            surf_rsem.at[4 + slot],
            peer * 4 + near,
        )

    for step in range(1, 4):
        near_copy(step, near).start()
    mid = surf_own[...]
    for step in range(1, 4):
        near_copy(step, (near + step) % 4).wait_recv()
        mid = mid + surf_recv[(near + step) % 4]
    surf_recv[4 + far] = mid
    for step in range(1, chunk_count):
        wide_copy(step, far).start()
    for step in range(1, chunk_count):
        wide_copy(step, (far + step) % chunk_count).wait_recv()
    total = surf_recv[4]
    for step in range(1, chunk_count):
        total = total + surf_recv[4 + step]
    total = total / (columns // 2)
    total_ref[...] = total
    out_ref[...] = total_ref[pl.ds(me, 1), :] / jnp.max(total)

    @pl.loop(1, devices)
    def _(step):
        peer = (me + step) % devices
        send(
            gram_part.at[pl.ds(pl.multiple_of(peer * 8, 8), 8), :],
            gram_recv.at[me],
            gram_ssem.at[peer],
            gram_rsem.at[me],
            peer,
        ).wait_send()
        send(
            gram_own, gram_full.at[own_rows, :], full_ssem.at[peer], full_rsem.at[me], peer
        ).wait_send()
        send(
            trace_send.at[peer], trace_recv.at[me], trace_ssem.at[peer], trace_rsem.at[me], peer
        ).wait_send()

    for step in range(1, 4):
        near_copy(step, near).wait_send()
    for step in range(1, chunk_count):
        wide_copy(step, far).wait_send()

    @pl.loop(0, chunk_count)
    def _(chunk):
        core_copy(chunk).wait_send()
        side_copy(chunk).wait_send()

        @pl.when(chunk != far)
        def _():
            far_copy(chunk, far).wait_send()


def per_device_fused(
    snapshots, freq_bins, mode_shapes, mode_counts, wavenumbers, source_modes, segment_owner
):
    devices = lax.axis_size("chan")
    snap_count, channels, samples = snapshots.shape
    segs, modes, depths = source_modes.shape
    blocks = segment_owner.shape[0]
    freqs = freq_bins.shape[0]
    columns = 2 * freqs
    half = math.isqrt(samples)
    rows = blocks * modes
    f32, bf16 = jnp.float32, jnp.bfloat16
    ranges_total = blocks * RPB
    dma = pltpu.SemaphoreType.DMA((devices,))
    vmem = pl.BlockSpec(memory_space=pltpu.VMEM)
    few = pltpu.SemaphoreType.DMA((devices // 4,))
    return pl.pallas_call(
        functools.partial(fused_kernel, devices),
        out_shape=jax.ShapeDtypeStruct((1, depths), f32),
        in_specs=[pl.BlockSpec(memory_space=pltpu.HBM)] * 7,
        out_specs=vmem,
        scratch_shapes=[
            pltpu.VMEM((freqs // LANES, LANES), jnp.int32),
            pltpu.VMEM((segs, modes, channels), bf16),
            pltpu.SMEM((segs,), jnp.int32),
            pltpu.VMEM((segs, modes, LANES), f32),
            pltpu.VMEM((segs, modes, depths), f32),
            pltpu.SMEM((blocks,), jnp.int32),
            pltpu.VMEM((snap_count * channels, samples), bf16),
            pltpu.VMEM((samples, 256), bf16),
            pltpu.VMEM((half, columns), f32),
            pltpu.VMEM((half, columns), f32),
            pltpu.VMEM((half, columns), f32),
            pltpu.VMEM((half, columns), f32),
            pltpu.VMEM((devices // 4, 2, rows, LANES), f32),
            pltpu.VMEM((devices // 4, 2, rows, LANES), bf16),
            pltpu.VMEM((devices // 4, 2, rows, LANES), bf16),
            pltpu.VMEM((devices // 4, rows, LANES), f32),
            pltpu.VMEM((devices // 4, rows, LANES), bf16),
            pltpu.VMEM((devices // 4, rows, LANES), bf16),
            pltpu.VMEM((rows, LANES), f32),
            pltpu.VMEM((devices // 4, rows, LANES), bf16),
            pltpu.VMEM((devices // 4, rows, LANES), bf16),
            pltpu.VMEM((devices, 1, LANES), f32),
            pltpu.VMEM((devices, 1, LANES), f32),
            pltpu.VMEM((devices * 8, LANES), f32),
            pltpu.VMEM((devices, 8, LANES), f32),
            pltpu.VMEM((8, LANES), f32),
            pltpu.VMEM((devices * 8, LANES), f32),
            pltpu.VMEM((modes * modes, LANES), bf16),
            pltpu.VMEM((modes * modes, LANES), bf16),
            pltpu.VMEM((ranges_total, depths), f32),
            pltpu.VMEM((4 + devices // 4, ranges_total, depths), f32),
            pltpu.VMEM((ranges_total, depths), f32),
            pltpu.SemaphoreType.DMA((7,)),
        ]
        + [few] * 6
        + [dma] * 8,
        compiler_params=pltpu.CompilerParams(
            collective_id=0, has_side_effects=True, vmem_limit_bytes=62 * 2**20
        ),
    )(
        freq_bins.reshape(freqs // LANES, LANES),
        snapshots.reshape(snap_count * channels, samples),
        mode_shapes,
        mode_counts,
        wavenumbers,
        source_modes,
        segment_owner,
    )


def per_device(*args):
    snapshots, freq_bins, mode_shapes, _, _, source_modes, segment_owner = args
    devices = lax.axis_size("chan")
    blocks = segment_owner.shape[0]
    freqs = freq_bins.shape[0]
    modes, depths = source_modes.shape[1:]
    fits = (
        snapshots.shape[0] == 2
        and 2 * 2 * freqs == devices * LANES
        and 4 * freqs // devices == LANES
        and blocks * RPB == devices
        and blocks * modes * modes == devices * 8 * LANES
        and 2 * modes == LANES
        and depths == LANES
        and math.isqrt(snapshots.shape[2]) ** 2 == snapshots.shape[2]
    )
    return per_device_fused(*args) if fits else per_device_plain(*args)


def solution(mesh):
    return jax.shard_map(
        per_device,
        mesh=mesh,
        in_specs=(P("groups", "chan", None), P(), P(None, None, "chan"), P(), P(), P(), P()),
        out_specs=P(("groups", "chan"), None),
        check_vma=False,
    )
```

```python
import functools
import math

import jax
import jax.numpy as jnp
from jax import lax
from jax.experimental import pallas as pl
from jax.experimental.pallas import tpu as pltpu
from jax.sharding import PartitionSpec as P

F = 512
RPB = 4


range_start = 1.0
range_step = 0.01


def dft_table(freq_bins, samples):
    sample_ids = jnp.arange(samples, dtype=jnp.int32)
    residue = freq_bins[:, None] * sample_ids[None, :] % samples
    angles = residue.astype(jnp.float32) * (2.0 * jnp.pi / samples)
    return jnp.stack([jnp.cos(angles), -jnp.sin(angles)]).astype(jnp.bfloat16)


def surface_terms(
    proj_flat,
    gram_rounded,
    traces,
    waves,
    source_modes,
    mode_counts,
    segment_owner,
    ranges_per_block,
    freq_total,
):
    segs, modes, depths = source_modes.shape
    freqs = proj_flat.shape[0]
    snaps = proj_flat.shape[2]
    highest = lax.Precision.HIGHEST
    proj_four = proj_flat.reshape(freqs, 2, snaps, segs, modes)
    proj_real = proj_four[:, 0]
    proj_imag = proj_four[:, 1]
    upper = jnp.concatenate([proj_real, proj_imag], axis=-1)
    lower = jnp.concatenate([proj_imag, -proj_real], axis=-1)
    coupling = jnp.concatenate([upper, lower], axis=1)
    coupling = jnp.transpose(coupling, (2, 0, 1, 3)).astype(jnp.float32)
    zero_block = jnp.zeros_like(gram_rounded)
    gram_double = jnp.concatenate(
        [
            jnp.concatenate([gram_rounded, zero_block], axis=2),
            jnp.concatenate([zero_block, gram_rounded], axis=2),
        ],
        axis=1,
    ).astype(jnp.float32)
    active = (jnp.arange(modes, dtype=jnp.int32)[None, :] < mode_counts[:, None]).astype(
        jnp.float32
    )
    masked = jnp.transpose(source_modes * active[:, :, None], (0, 2, 1))
    mode_double = jnp.concatenate([masked, masked], axis=-1)
    wave_t = jnp.transpose(waves, (0, 2, 1))
    wave_double = jnp.concatenate([wave_t, wave_t], axis=-1)
    lanes = jnp.arange(2 * modes, dtype=jnp.int32) < modes
    seg_ids = jnp.arange(segs, dtype=jnp.int32)
    blocks = segment_owner.shape[0]

    def one_block(items):
        block_id, owner = items
        pick = (seg_ids == owner).astype(jnp.float32)
        wave_block = jnp.einsum("s,sfm->fm", pick, wave_double, precision=highest)
        mode_block = jnp.einsum("s,szm->zm", pick, mode_double, precision=highest)
        coupling_block = jnp.einsum("s,sfkm->fkm", pick, coupling, precision=highest).astype(
            jnp.bfloat16
        )
        gram_block = jnp.einsum("s,smn->mn", pick, gram_double, precision=highest).astype(
            jnp.bfloat16
        )
        range_ids = block_id * ranges_per_block + jnp.arange(ranges_per_block, dtype=jnp.int32)
        ranges = range_start + range_step * range_ids.astype(jnp.float32)
        phases = wave_block[:, None, :] * ranges[None, :, None]
        trig = jnp.where(lanes[None, None, :], jnp.cos(phases), jnp.sin(phases))
        amplitude = mode_block[None, None, :, :] / jnp.sqrt(phases)[:, :, None, :]
        cells = ranges_per_block * depths
        replica = (
            (amplitude * trig[:, :, None, :]).reshape(freqs, cells, 2 * modes).astype(jnp.bfloat16)
        )
        beams = jnp.einsum(
            "fkm,fcm->fkc", coupling_block, replica, preferred_element_type=jnp.float32
        )
        powers = jnp.sum(beams * beams, axis=1)
        mapped = jnp.einsum("fcm,mn->fcn", replica, gram_block, preferred_element_type=jnp.float32)
        weight_norm = jnp.sum(replica.astype(jnp.float32) * mapped, axis=-1)
        bartlett = powers / (snaps * traces[:, None] * weight_norm)
        return (jnp.sum(bartlett, axis=0) / freq_total).reshape(ranges_per_block, depths)

    block_ids = jnp.arange(blocks, dtype=jnp.int32)
    parts = lax.map(one_block, (block_ids, segment_owner))
    return parts.reshape(blocks * ranges_per_block, depths)


def per_device_plain(
    snapshots, freq_bins, mode_shapes, mode_counts, wavenumbers, source_modes, segment_owner
):
    devices_chan = lax.axis_size("chan")
    samples = snapshots.shape[2]
    segs = mode_shapes.shape[0]
    modes = mode_shapes.shape[1]
    local_freqs = F // devices_chan
    table_values = dft_table(freq_bins, samples)
    spectra = jnp.einsum(
        "cft,lht->cflh", table_values, snapshots, preferred_element_type=jnp.float32
    ).astype(jnp.bfloat16)
    moved = lax.all_to_all(spectra, "chan", split_axis=1, concat_axis=3, tiled=True)
    traces = jnp.sum(jnp.square(moved.astype(jnp.float32)), axis=(0, 2, 3))
    piece = lax.all_gather(mode_shapes, "chan", axis=2, tiled=True)
    flat_piece = piece.reshape(segs * modes, piece.shape[2])
    projections = jnp.einsum("cflh,kh->fclk", moved, flat_piece, preferred_element_type=jnp.float32)
    proj_rounded = projections.astype(jnp.bfloat16)
    local_gram = jnp.einsum(
        "smh,snh->smn", mode_shapes, mode_shapes, preferred_element_type=jnp.float32
    )
    gram = lax.psum(local_gram.reshape(segs, modes * modes), "chan")
    gram_rounded = gram.reshape(segs, modes, modes).astype(jnp.bfloat16)
    first_freq = lax.axis_index("chan") * local_freqs
    local_waves = lax.dynamic_slice_in_dim(wavenumbers, first_freq, local_freqs, 2)
    partial_surface = surface_terms(
        proj_rounded,
        gram_rounded,
        traces,
        local_waves,
        source_modes,
        mode_counts,
        segment_owner,
        RPB,
        F,
    )
    own_rows = partial_surface.shape[0] // devices_chan
    total_surface = lax.psum(partial_surface, "chan")
    highest_value = jnp.max(total_surface)
    own_surface = lax.dynamic_slice_in_dim(
        total_surface, lax.axis_index("chan") * own_rows, own_rows, 0
    )
    return own_surface / highest_value


LANES = 128
MESH = pl.DeviceIdType.MESH
HIGHEST = lax.Precision.HIGHEST


def sincos_small(x):
    y = x * x
    sine = x + x * y * (
        -1.6666667e-1 + y * (8.3333333e-3 + y * (-1.9841270e-4 + y * 2.7557319e-6))
    )
    cosine = 1.0 + y * (
        -0.5 + y * (4.1666667e-2 + y * (-1.3888889e-3 + y * (2.4801587e-5 - y * 2.7557319e-7)))
    )
    return sine, cosine


def turn(quadrant, sine, cosine):
    odd = (quadrant & 1) == 1
    c = jnp.where(odd, sine, cosine)
    s = jnp.where(odd, cosine, sine)
    return (
        jnp.where((quadrant & 2) != 0, -s, s),
        jnp.where(((quadrant + 1) & 2) != 0, -c, c),
    )


def sincos_bins(q, samples):
    quarter = samples // 4
    q = q & (samples - 1)
    quadrant = (q + quarter // 2) // quarter
    x = (q - quadrant * quarter).astype(jnp.float32) * (2.0 * math.pi / samples)
    return turn(quadrant, *sincos_small(x))


def sincos_wide(x):
    n = jnp.floor(x * (2.0 / math.pi) + 0.5)
    y = ((x - n * 1.5703125) - n * 4.837512969970703125e-4) - n * 7.54978995489188216e-8
    return turn(n.astype(jnp.int32), *sincos_small(y))


def fused_kernel(
    devices,
    freq_hbm,
    snaps_hbm,
    modes_hbm,
    counts_hbm,
    waves_hbm,
    source_hbm,
    owner_hbm,
    out_ref,
    freq_ref,
    modes_ref,
    counts_ref,
    waves_ref,
    modes_source_ref,
    owner_ref,
    snaps,
    table,
    cos_a,
    sin_a,
    cos_b,
    sin_b,
    kept,
    core_send,
    core_recv,
    side_kept,
    side_send,
    side_recv,
    far_kept,
    far_send,
    far_recv,
    trace_send,
    trace_recv,
    gram_part,
    gram_recv,
    gram_own,
    gram_full,
    terms_a,
    terms_b,
    surf_own,
    surf_recv,
    total_ref,
    load_sem,
    core_ssem,
    core_rsem,
    side_ssem,
    side_rsem,
    far_ssem,
    far_rsem,
    trace_ssem,
    trace_rsem,
    gram_ssem,
    gram_rsem,
    full_ssem,
    full_rsem,
    surf_ssem,
    surf_rsem,
):
    me = lax.axis_index("chan")
    snap_count = 2
    samples = snaps_hbm.shape[1]
    channels = snaps_hbm.shape[0] // snap_count
    blocks = owner_ref.shape[0]
    modes, depths = modes_source_ref.shape[1:]
    columns = 2 * freq_ref.shape[0] * freq_ref.shape[1]
    core = me % 2
    side = (me // 2) % 2
    far = me // 4
    other_core = far * 4 + side * 2 + 1 - core
    other_side = far * 4 + (1 - side) * 2 + core
    width = table.shape[1]
    f32 = jnp.float32

    window = pl.ds(pl.multiple_of((me // 4) * LANES, LANES), LANES)
    loads = [
        pltpu.make_async_copy(src, dst, load_sem.at[n])
        for n, (src, dst) in enumerate(
            [
                (freq_hbm, freq_ref),
                (owner_hbm, owner_ref),
                (counts_hbm, counts_ref),
                (modes_hbm, modes_ref),
                (source_hbm, modes_source_ref),
                (waves_hbm.at[:, :, window], waves_ref),
                (snaps_hbm, snaps),
            ]
        )
    ]
    for load in loads:
        load.start()

    barrier = pltpu.get_barrier_semaphore()
    for step in range(1, devices):
        pl.semaphore_signal(
            barrier, inc=1, device_id={"chan": (me + step) % devices}, device_id_type=MESH
        )

    def send(src, dst, ssem, rsem, peer):
        return pltpu.make_async_remote_copy(
            src_ref=src,
            dst_ref=dst,
            send_sem=ssem,
            recv_sem=rsem,
            device_id={"chan": peer},
            device_id_type=MESH,
        )

    half = cos_a.shape[0]
    loads[0].wait()
    lane = lax.broadcasted_iota(jnp.int32, (1, LANES), 1)
    quarter = LANES // 4
    group = lane // quarter
    pieces = []
    for piece in range(columns // LANES):
        here = freq_ref[piece // 2 : piece // 2 + 1, :]
        shifts = (2 * quarter, 3 * quarter, 3 * quarter, 0) if piece % 2 else (0, quarter, quarter, 2 * quarter)
        turned = [pltpu.roll(here, n, 1) if n else here for n in shifts]
        pieces.append(
            jnp.where(
                group == 0,
                turned[0],
                jnp.where(group == 1, turned[1], jnp.where(group == 2, turned[2], turned[3])),
            )
        )
    freqs = jnp.concatenate(pieces, axis=1)
    column = lax.broadcasted_iota(jnp.int32, (half, columns), 1)
    row = lax.broadcasted_iota(jnp.int32, (half, columns), 0)
    part_size = columns // devices // 2
    shift = ((column // part_size) & 1) * (samples // 4)
    sin_v, cos_v = sincos_bins(freqs * (row * half) + shift, samples)
    sin_a[...] = sin_v
    cos_a[...] = cos_v
    sin_v, cos_v = sincos_bins(freqs * row, samples)
    sin_b[...] = sin_v
    cos_b[...] = cos_v

    for load in loads[1:4]:
        load.wait()
    owners = [owner_ref[block] for block in range(blocks)]
    shapes = jnp.concatenate([modes_ref[owner] for owner in owners], axis=0)
    inner = lax.dot_general(shapes, shapes, (((1,), (1,)), ((), ())), preferred_element_type=f32)
    low_half = lax.broadcasted_iota(jnp.int32, (modes, LANES), 1) < modes
    for pair in range(blocks // 2):
        base = pair * LANES
        gram_part[pair * modes : (pair + 1) * modes, :] = jnp.where(
            low_half,
            inner[base : base + modes, base : base + LANES],
            inner[base + modes : base + LANES, base : base + LANES],
        )
    pl.semaphore_wait(barrier, devices - 1)

    @pl.loop(1, devices)
    def _(step):
        peer = (me + step) % devices
        send(
            gram_part.at[pl.ds(pl.multiple_of(peer * 8, 8), 8), :],
            gram_recv.at[me],
            gram_ssem.at[peer],
            gram_rsem.at[me],
            peer,
        ).start()

    gram_recv[me] = gram_part[pl.ds(pl.multiple_of(me * 8, 8), 8), :]

    for load in loads[4:]:
        load.wait()
    own_rows = pl.ds(pl.multiple_of(me * 8, 8), 8)
    per_chunk = width // (columns // devices)
    chunk_count = columns // width
    wide_low = lax.broadcasted_iota(jnp.int32, (blocks * modes, LANES), 1) < LANES // 2
    thin_low = wide_low[:8]

    def core_copy(chunk):
        return send(
            core_send.at[chunk], core_recv.at[chunk], core_ssem.at[chunk], core_rsem.at[chunk], other_core
        )

    def side_copy(chunk):
        return send(
            side_send.at[chunk], side_recv.at[chunk], side_ssem.at[chunk], side_rsem.at[chunk], other_side
        )

    def far_copy(chunk, slot):
        peer = chunk * 4 + side * 2 + core
        return send(far_send.at[chunk], far_recv.at[slot], far_ssem.at[chunk], far_rsem.at[slot], peer)

    def chunk_of(step):
        return (far + 1 + step) % chunk_count

    def make(step):
        chunk = chunk_of(step)
        cols = pl.ds(pl.multiple_of(chunk * width, width), width)
        cb = cos_b[:, cols]
        sb = sin_b[:, cols]

        def build(first):
            for a in range(first, first + half // 4):
                ca = cos_a[a : a + 1, cols]
                sa = sin_a[a : a + 1, cols]
                table[a * half : (a + 1) * half, :] = (ca * cb - sa * sb).astype(jnp.bfloat16)

        parts = []
        sums = []
        build(0)
        both = None
        for quart in range(4):
            rows = slice(quart * samples // 4, (quart + 1) * samples // 4)
            term = jnp.dot(snaps[:, rows], table[rows, :], preferred_element_type=f32)
            if quart < 3:
                build((quart + 1) * half // 4)
            both = term if both is None else both + term
        both = both.astype(jnp.bfloat16)
        for snap in range(snap_count):
            spectra = both[snap * channels : (snap + 1) * channels]
            wide = spectra.astype(f32)
            sums.append(jnp.broadcast_to(jnp.sum(wide * wide, axis=0, keepdims=True), (8, width)))
            parts.append(jnp.dot(shapes, spectra, preferred_element_type=f32))
        for pair in range(per_chunk // 2):
            lanes = slice(pair * LANES, (pair + 1) * LANES)
            p0, p1 = parts[0][:, lanes], parts[1][:, lanes]
            t0, t1 = sums[0][:, lanes], sums[1][:, lanes]
            first = jnp.where(wide_low, p0, pltpu.roll(p1, LANES // 2, 1))
            second = jnp.where(wide_low, pltpu.roll(p0, LANES // 2, 1), p1)
            kept[chunk, pair] = jnp.where(core == 0, first, second)
            core_send[chunk, pair] = jnp.where(core == 0, second, first).astype(jnp.bfloat16)
            dest = chunk * per_chunk + 2 * pair
            trace_send[dest] = jnp.where(thin_low, t0, pltpu.roll(t1, LANES // 2, 1))[:1]
            trace_send[dest + 1] = jnp.where(thin_low, pltpu.roll(t0, LANES // 2, 1), t1)[:1]
        core_copy(chunk).start()
        for k in range(per_chunk):
            dest = chunk * per_chunk + k

            @pl.when(dest != me)
            def _():
                send(
                    trace_send.at[dest],
                    trace_recv.at[me],
                    trace_ssem.at[dest],
                    trace_rsem.at[me],
                    dest,
                ).start()

    def add_core(step):
        chunk = chunk_of(step)
        core_copy(chunk).wait_recv()
        side_kept[chunk] = kept[chunk, side] + core_recv[chunk, side].astype(f32)
        side_send[chunk] = (kept[chunk, 1 - side] + core_recv[chunk, 1 - side].astype(f32)).astype(
            jnp.bfloat16
        )
        side_copy(chunk).start()

    def add_side(step, keep=False):
        chunk = chunk_of(step)
        side_copy(chunk).wait_recv()
        total = side_kept[chunk] + side_recv[chunk].astype(f32)
        if keep:
            far_kept[...] = total
        else:
            far_send[chunk] = total.astype(jnp.bfloat16)
            far_copy(chunk, far).start()

    def gram_share():
        @pl.loop(1, devices)
        def _(step):
            peer = (me + step) % devices
            send(
                gram_part.at[pl.ds(0, 8), :],
                gram_recv.at[peer],
                gram_ssem.at[peer],
                gram_rsem.at[peer],
                peer,
            ).wait_recv()

        gram_own[...] = jnp.sum(gram_recv[...], axis=0)
        gram_full[own_rows, :] = gram_own[...]

        @pl.loop(1, devices)
        def _(step):
            peer = (me + step) % devices
            send(
                gram_own, gram_full.at[own_rows, :], full_ssem.at[peer], full_rsem.at[me], peer
            ).start()

    last = chunk_count - 1

    @pl.loop(0, chunk_count)
    def _(step):
        make(step)

        @pl.when(step == 0)
        def _():
            gram_share()

        @pl.when(step >= 1)
        def _():
            add_core(step - 1)

        @pl.when(step >= 2)
        def _():
            add_side(step - 2)

    add_core(last)
    add_side(last - 1)
    trace_recv[me] = trace_send[me]

    @pl.loop(1, devices)
    def _(step):
        peer = (me + step) % devices
        send(
            gram_own,
            gram_full.at[pl.ds(pl.multiple_of(peer * 8, 8), 8), :],
            full_ssem.at[peer],
            full_rsem.at[peer],
            peer,
        ).wait_recv()

    gram = gram_full[...].astype(jnp.bfloat16).astype(f32)
    tile = 16
    first_tile = (lax.broadcasted_iota(jnp.int32, gram.shape, 0) % modes) // tile
    second_tile = (lax.broadcasted_iota(jnp.int32, gram.shape, 1) % modes) // tile
    gram = jnp.where(first_tile > second_tile, 2.0 * gram, gram)
    pairs = sum(tile * (modes - start) for start in range(0, modes, tile))
    wide_lane = lax.broadcasted_iota(jnp.int32, (modes, LANES), 1)
    mode_ids = lax.broadcasted_iota(jnp.int32, (modes, depths), 0)
    sources = []
    waves_sin = []
    waves_cos = []
    norms = []
    for block in range(blocks):
        wave = waves_ref[owners[block]]
        wave = jnp.where(wide_lane // quarter == me % 4, wave, 0.0)
        wave = wave + pltpu.roll(wave, quarter, 1)
        wave = wave + pltpu.roll(wave, 2 * quarter, 1)
        range_ids = block * RPB + wide_lane // quarter
        phases = wave * (range_start + range_step * range_ids.astype(f32))
        sine, cosine = sincos_wide(phases)
        scale = 1.0 / jnp.sqrt(phases)
        sine, cosine = sine * scale, cosine * scale
        waves_sin.append(sine)
        waves_cos.append(cosine)
        source = jnp.where(
            mode_ids < counts_ref[owners[block]], modes_source_ref[owners[block]], 0.0
        )
        sources.append(source)
        base = (block // 2) * modes
        filled = 0
        for m in range(modes):
            low = m // tile * tile
            lane = (block % 2) * modes + m
            at = slice(filled, filled + modes - low)
            filled += modes - low
            terms_a[at, :] = (
                cosine[m : m + 1] * cosine[low:] + sine[m : m + 1] * sine[low:]
            ).astype(jnp.bfloat16)
            terms_b[at, :] = (
                gram[base + low : base + modes, lane : lane + 1] * (source[m : m + 1] * source[low:])
            ).astype(jnp.bfloat16)
        norms.append(
            lax.dot_general(
                terms_a[:pairs],
                terms_b[:pairs],
                (((0,), (0,)), ((), ())),
                preferred_element_type=f32,
            )
        )

    add_side(last, keep=True)

    @pl.loop(1, devices)
    def _(step):
        peer = (me + step) % devices
        send(
            trace_send.at[peer],
            trace_recv.at[peer],
            trace_ssem.at[peer],
            trace_rsem.at[peer],
            peer,
        ).wait_recv()

    proj = far_kept[...]
    for step in range(1, chunk_count):
        slot = (far + step) % chunk_count
        far_copy(slot, slot).wait_recv()
        proj = proj + far_recv[slot].astype(f32)
    proj = proj.astype(jnp.bfloat16)
    trace = jnp.broadcast_to(jnp.sum(trace_recv[...], axis=0), (8, LANES))
    trace = trace + pltpu.roll(trace, 2 * quarter, 1)
    trace = trace + pltpu.roll(trace, quarter, 1)
    level = (1.0 / jnp.sqrt(snap_count * trace))[:1]

    pick_in = lax.broadcasted_iota(jnp.int32, (LANES, 4 * LANES), 0)
    pick_out = lax.broadcasted_iota(jnp.int32, (LANES, 4 * LANES), 1)
    pick = (pick_in // quarter == pick_out // LANES) & (pick_in % quarter == pick_out % quarter)
    spread = jnp.dot(proj, pick.astype(f32).astype(jnp.bfloat16), preferred_element_type=f32)
    for block in range(blocks):
        sine, cosine = waves_sin[block] * level, waves_cos[block] * level
        rows = slice(block * modes, (block + 1) * modes)
        coupled = []
        for snap in range(snap_count):
            real = spread[rows, (2 * snap) * LANES : (2 * snap + 1) * LANES]
            imag = spread[rows, (2 * snap + 1) * LANES : (2 * snap + 2) * LANES]
            coupled.append(cosine * real + sine * imag)
            coupled.append(cosine * imag - sine * real)
        coupled = jnp.concatenate(coupled, axis=1)
        coupled_high = coupled.astype(jnp.bfloat16)
        coupled_low = (coupled - coupled_high.astype(f32)).astype(jnp.bfloat16)
        source = sources[block]
        source_high = source.astype(jnp.bfloat16)
        source_low = (source - source_high.astype(f32)).astype(jnp.bfloat16)
        beams = lax.dot_general(
            jnp.concatenate([coupled_high, coupled_low, coupled_high], axis=0),
            jnp.concatenate([source_high, source_high, source_low], axis=0),
            (((0,), (0,)), ((), ())),
            preferred_element_type=f32,
        )
        squares = beams * beams
        power = (
            squares[:LANES]
            + squares[LANES : 2 * LANES]
            + squares[2 * LANES : 3 * LANES]
            + squares[3 * LANES :]
        )
        ratio = power / norms[block]
        for j in range(4):
            surf_own[block * 4 + j : block * 4 + j + 1, :] = jnp.sum(
                ratio[j * quarter : (j + 1) * quarter], axis=0, keepdims=True
            )

    surf_recv[me] = surf_own[...]

    @pl.loop(1, devices)
    def _(step):
        peer = (me + step) % devices
        send(surf_own, surf_recv.at[me], surf_ssem.at[peer], surf_rsem.at[me], peer).start()

    @pl.loop(1, devices)
    def _(step):
        peer = (me + step) % devices
        send(
            gram_part.at[pl.ds(pl.multiple_of(peer * 8, 8), 8), :],
            gram_recv.at[me],
            gram_ssem.at[peer],
            gram_rsem.at[me],
            peer,
        ).wait_send()
        send(
            gram_own, gram_full.at[own_rows, :], full_ssem.at[peer], full_rsem.at[me], peer
        ).wait_send()
        send(
            trace_send.at[peer], trace_recv.at[me], trace_ssem.at[peer], trace_rsem.at[me], peer
        ).wait_send()

    @pl.loop(0, chunk_count)
    def _(chunk):
        core_copy(chunk).wait_send()
        side_copy(chunk).wait_send()

        @pl.when(chunk != far)
        def _():
            far_copy(chunk, far).wait_send()

    @pl.loop(1, devices)
    def _(step):
        peer = (me + step) % devices
        send(surf_own, surf_recv.at[peer], surf_ssem.at[peer], surf_rsem.at[peer], peer).wait()

    total = jnp.sum(surf_recv[...], axis=0) / (columns // 2)
    total_ref[...] = total
    out_ref[...] = total_ref[pl.ds(me, 1), :] / jnp.max(total)


def per_device_fused(
    snapshots, freq_bins, mode_shapes, mode_counts, wavenumbers, source_modes, segment_owner
):
    devices = lax.axis_size("chan")
    snap_count, channels, samples = snapshots.shape
    segs, modes, depths = source_modes.shape
    blocks = segment_owner.shape[0]
    freqs = freq_bins.shape[0]
    columns = 2 * freqs
    half = math.isqrt(samples)
    rows = blocks * modes
    f32, bf16 = jnp.float32, jnp.bfloat16
    ranges_total = blocks * RPB
    dma = pltpu.SemaphoreType.DMA((devices,))
    vmem = pl.BlockSpec(memory_space=pltpu.VMEM)
    few = pltpu.SemaphoreType.DMA((devices // 4,))
    return pl.pallas_call(
        functools.partial(fused_kernel, devices),
        out_shape=jax.ShapeDtypeStruct((1, depths), f32),
        in_specs=[pl.BlockSpec(memory_space=pltpu.HBM)] * 7,
        out_specs=vmem,
        scratch_shapes=[
            pltpu.VMEM((freqs // LANES, LANES), jnp.int32),
            pltpu.VMEM((segs, modes, channels), bf16),
            pltpu.SMEM((segs,), jnp.int32),
            pltpu.VMEM((segs, modes, LANES), f32),
            pltpu.VMEM((segs, modes, depths), f32),
            pltpu.SMEM((blocks,), jnp.int32),
            pltpu.VMEM((snap_count * channels, samples), bf16),
            pltpu.VMEM((samples, 256), bf16),
            pltpu.VMEM((half, columns), f32),
            pltpu.VMEM((half, columns), f32),
            pltpu.VMEM((half, columns), f32),
            pltpu.VMEM((half, columns), f32),
            pltpu.VMEM((devices // 4, 2, rows, LANES), f32),
            pltpu.VMEM((devices // 4, 2, rows, LANES), bf16),
            pltpu.VMEM((devices // 4, 2, rows, LANES), bf16),
            pltpu.VMEM((devices // 4, rows, LANES), f32),
            pltpu.VMEM((devices // 4, rows, LANES), bf16),
            pltpu.VMEM((devices // 4, rows, LANES), bf16),
            pltpu.VMEM((rows, LANES), f32),
            pltpu.VMEM((devices // 4, rows, LANES), bf16),
            pltpu.VMEM((devices // 4, rows, LANES), bf16),
            pltpu.VMEM((devices, 1, LANES), f32),
            pltpu.VMEM((devices, 1, LANES), f32),
            pltpu.VMEM((devices * 8, LANES), f32),
            pltpu.VMEM((devices, 8, LANES), f32),
            pltpu.VMEM((8, LANES), f32),
            pltpu.VMEM((devices * 8, LANES), f32),
            pltpu.VMEM((modes * modes, LANES), bf16),
            pltpu.VMEM((modes * modes, LANES), bf16),
            pltpu.VMEM((ranges_total, depths), f32),
            pltpu.VMEM((devices, ranges_total, depths), f32),
            pltpu.VMEM((ranges_total, depths), f32),
            pltpu.SemaphoreType.DMA((7,)),
        ]
        + [few] * 6
        + [dma] * 8,
        compiler_params=pltpu.CompilerParams(
            collective_id=0, has_side_effects=True, vmem_limit_bytes=62 * 2**20
        ),
    )(
        freq_bins.reshape(freqs // LANES, LANES),
        snapshots.reshape(snap_count * channels, samples),
        mode_shapes,
        mode_counts,
        wavenumbers,
        source_modes,
        segment_owner,
    )


def per_device(*args):
    snapshots, freq_bins, mode_shapes, _, _, source_modes, segment_owner = args
    devices = lax.axis_size("chan")
    blocks = segment_owner.shape[0]
    freqs = freq_bins.shape[0]
    modes, depths = source_modes.shape[1:]
    fits = (
        snapshots.shape[0] == 2
        and 2 * 2 * freqs == devices * LANES
        and 4 * freqs // devices == LANES
        and blocks * RPB == devices
        and blocks * modes * modes == devices * 8 * LANES
        and 2 * modes == LANES
        and depths == LANES
        and math.isqrt(snapshots.shape[2]) ** 2 == snapshots.shape[2]
    )
    return per_device_fused(*args) if fits else per_device_plain(*args)


def solution(mesh):
    return jax.shard_map(
        per_device,
        mesh=mesh,
        in_specs=(P("groups", "chan", None), P(), P(None, None, "chan"), P(), P(), P(), P()),
        out_specs=P(("groups", "chan"), None),
        check_vma=False,
    )
```

```python
import functools
import math

import jax
import jax.numpy as jnp
from jax import lax
from jax.experimental import pallas as pl
from jax.experimental.pallas import tpu as pltpu
from jax.sharding import PartitionSpec as P

F = 512
RPB = 4


range_start = 1.0
range_step = 0.01


def dft_table(freq_bins, samples):
    sample_ids = jnp.arange(samples, dtype=jnp.int32)
    residue = freq_bins[:, None] * sample_ids[None, :] % samples
    angles = residue.astype(jnp.float32) * (2.0 * jnp.pi / samples)
    return jnp.stack([jnp.cos(angles), -jnp.sin(angles)]).astype(jnp.bfloat16)


def surface_terms(
    proj_flat,
    gram_rounded,
    traces,
    waves,
    source_modes,
    mode_counts,
    segment_owner,
    ranges_per_block,
    freq_total,
):
    segs, modes, depths = source_modes.shape
    freqs = proj_flat.shape[0]
    snaps = proj_flat.shape[2]
    highest = lax.Precision.HIGHEST
    proj_four = proj_flat.reshape(freqs, 2, snaps, segs, modes)
    proj_real = proj_four[:, 0]
    proj_imag = proj_four[:, 1]
    upper = jnp.concatenate([proj_real, proj_imag], axis=-1)
    lower = jnp.concatenate([proj_imag, -proj_real], axis=-1)
    coupling = jnp.concatenate([upper, lower], axis=1)
    coupling = jnp.transpose(coupling, (2, 0, 1, 3)).astype(jnp.float32)
    zero_block = jnp.zeros_like(gram_rounded)
    gram_double = jnp.concatenate(
        [
            jnp.concatenate([gram_rounded, zero_block], axis=2),
            jnp.concatenate([zero_block, gram_rounded], axis=2),
        ],
        axis=1,
    ).astype(jnp.float32)
    active = (jnp.arange(modes, dtype=jnp.int32)[None, :] < mode_counts[:, None]).astype(
        jnp.float32
    )
    masked = jnp.transpose(source_modes * active[:, :, None], (0, 2, 1))
    mode_double = jnp.concatenate([masked, masked], axis=-1)
    wave_t = jnp.transpose(waves, (0, 2, 1))
    wave_double = jnp.concatenate([wave_t, wave_t], axis=-1)
    lanes = jnp.arange(2 * modes, dtype=jnp.int32) < modes
    seg_ids = jnp.arange(segs, dtype=jnp.int32)
    blocks = segment_owner.shape[0]

    def one_block(items):
        block_id, owner = items
        pick = (seg_ids == owner).astype(jnp.float32)
        wave_block = jnp.einsum("s,sfm->fm", pick, wave_double, precision=highest)
        mode_block = jnp.einsum("s,szm->zm", pick, mode_double, precision=highest)
        coupling_block = jnp.einsum("s,sfkm->fkm", pick, coupling, precision=highest).astype(
            jnp.bfloat16
        )
        gram_block = jnp.einsum("s,smn->mn", pick, gram_double, precision=highest).astype(
            jnp.bfloat16
        )
        range_ids = block_id * ranges_per_block + jnp.arange(ranges_per_block, dtype=jnp.int32)
        ranges = range_start + range_step * range_ids.astype(jnp.float32)
        phases = wave_block[:, None, :] * ranges[None, :, None]
        trig = jnp.where(lanes[None, None, :], jnp.cos(phases), jnp.sin(phases))
        amplitude = mode_block[None, None, :, :] / jnp.sqrt(phases)[:, :, None, :]
        cells = ranges_per_block * depths
        replica = (
            (amplitude * trig[:, :, None, :]).reshape(freqs, cells, 2 * modes).astype(jnp.bfloat16)
        )
        beams = jnp.einsum(
            "fkm,fcm->fkc", coupling_block, replica, preferred_element_type=jnp.float32
        )
        powers = jnp.sum(beams * beams, axis=1)
        mapped = jnp.einsum("fcm,mn->fcn", replica, gram_block, preferred_element_type=jnp.float32)
        weight_norm = jnp.sum(replica.astype(jnp.float32) * mapped, axis=-1)
        bartlett = powers / (snaps * traces[:, None] * weight_norm)
        return (jnp.sum(bartlett, axis=0) / freq_total).reshape(ranges_per_block, depths)

    block_ids = jnp.arange(blocks, dtype=jnp.int32)
    parts = lax.map(one_block, (block_ids, segment_owner))
    return parts.reshape(blocks * ranges_per_block, depths)


def per_device_plain(
    snapshots, freq_bins, mode_shapes, mode_counts, wavenumbers, source_modes, segment_owner
):
    devices_chan = lax.axis_size("chan")
    samples = snapshots.shape[2]
    segs = mode_shapes.shape[0]
    modes = mode_shapes.shape[1]
    local_freqs = F // devices_chan
    table_values = dft_table(freq_bins, samples)
    spectra = jnp.einsum(
        "cft,lht->cflh", table_values, snapshots, preferred_element_type=jnp.float32
    ).astype(jnp.bfloat16)
    moved = lax.all_to_all(spectra, "chan", split_axis=1, concat_axis=3, tiled=True)
    traces = jnp.sum(jnp.square(moved.astype(jnp.float32)), axis=(0, 2, 3))
    piece = lax.all_gather(mode_shapes, "chan", axis=2, tiled=True)
    flat_piece = piece.reshape(segs * modes, piece.shape[2])
    projections = jnp.einsum("cflh,kh->fclk", moved, flat_piece, preferred_element_type=jnp.float32)
    proj_rounded = projections.astype(jnp.bfloat16)
    local_gram = jnp.einsum(
        "smh,snh->smn", mode_shapes, mode_shapes, preferred_element_type=jnp.float32
    )
    gram = lax.psum(local_gram.reshape(segs, modes * modes), "chan")
    gram_rounded = gram.reshape(segs, modes, modes).astype(jnp.bfloat16)
    first_freq = lax.axis_index("chan") * local_freqs
    local_waves = lax.dynamic_slice_in_dim(wavenumbers, first_freq, local_freqs, 2)
    partial_surface = surface_terms(
        proj_rounded,
        gram_rounded,
        traces,
        local_waves,
        source_modes,
        mode_counts,
        segment_owner,
        RPB,
        F,
    )
    own_rows = partial_surface.shape[0] // devices_chan
    total_surface = lax.psum(partial_surface, "chan")
    highest_value = jnp.max(total_surface)
    own_surface = lax.dynamic_slice_in_dim(
        total_surface, lax.axis_index("chan") * own_rows, own_rows, 0
    )
    return own_surface / highest_value


LANES = 128
MESH = pl.DeviceIdType.MESH
HIGHEST = lax.Precision.HIGHEST


def sincos_small(x):
    y = x * x
    sine = x + x * y * (
        -1.6666667e-1 + y * (8.3333333e-3 + y * (-1.9841270e-4 + y * 2.7557319e-6))
    )
    cosine = 1.0 + y * (
        -0.5 + y * (4.1666667e-2 + y * (-1.3888889e-3 + y * (2.4801587e-5 - y * 2.7557319e-7)))
    )
    return sine, cosine


def turn(quadrant, sine, cosine):
    odd = (quadrant & 1) == 1
    c = jnp.where(odd, sine, cosine)
    s = jnp.where(odd, cosine, sine)
    return (
        jnp.where((quadrant & 2) != 0, -s, s),
        jnp.where(((quadrant + 1) & 2) != 0, -c, c),
    )


def sincos_bins(q, samples):
    quarter = samples // 4
    q = q & (samples - 1)
    quadrant = (q + quarter // 2) // quarter
    x = (q - quadrant * quarter).astype(jnp.float32) * (2.0 * math.pi / samples)
    return turn(quadrant, *sincos_small(x))


def sincos_wide(x):
    n = jnp.floor(x * (2.0 / math.pi) + 0.5)
    y = ((x - n * 1.5703125) - n * 4.837512969970703125e-4) - n * 7.54978995489188216e-8
    return turn(n.astype(jnp.int32), *sincos_small(y))


def fused_kernel(
    devices,
    freq_hbm,
    snaps_hbm,
    modes_hbm,
    counts_hbm,
    waves_hbm,
    source_hbm,
    owner_hbm,
    out_ref,
    freq_ref,
    modes_ref,
    counts_ref,
    waves_ref,
    modes_source_ref,
    owner_ref,
    snaps,
    table,
    cos_a,
    sin_a,
    cos_b,
    sin_b,
    kept,
    core_send,
    core_recv,
    side_kept,
    side_send,
    side_recv,
    far_kept,
    far_send,
    far_recv,
    trace_send,
    trace_recv,
    gram_part,
    gram_recv,
    gram_own,
    gram_full,
    terms_a,
    terms_b,
    surf_own,
    surf_recv,
    total_ref,
    load_sem,
    core_ssem,
    core_rsem,
    side_ssem,
    side_rsem,
    far_ssem,
    far_rsem,
    trace_ssem,
    trace_rsem,
    gram_ssem,
    gram_rsem,
    full_ssem,
    full_rsem,
    surf_ssem,
    surf_rsem,
):
    me = lax.axis_index("chan")
    snap_count = 2
    samples = snaps_hbm.shape[1]
    channels = snaps_hbm.shape[0] // snap_count
    blocks = owner_ref.shape[0]
    modes, depths = modes_source_ref.shape[1:]
    columns = 2 * freq_ref.shape[0] * freq_ref.shape[1]
    core = me % 2
    side = (me // 2) % 2
    far = me // 4
    other_core = far * 4 + side * 2 + 1 - core
    other_side = far * 4 + (1 - side) * 2 + core
    width = table.shape[1]
    f32 = jnp.float32

    window = pl.ds(pl.multiple_of((me // 4) * LANES, LANES), LANES)
    loads = [
        pltpu.make_async_copy(src, dst, load_sem.at[n])
        for n, (src, dst) in enumerate(
            [
                (freq_hbm, freq_ref),
                (owner_hbm, owner_ref),
                (counts_hbm, counts_ref),
                (modes_hbm, modes_ref),
                (source_hbm, modes_source_ref),
                (waves_hbm.at[:, :, window], waves_ref),
                (snaps_hbm, snaps),
            ]
        )
    ]
    for load in loads:
        load.start()

    barrier = pltpu.get_barrier_semaphore()
    for step in range(1, devices):
        pl.semaphore_signal(
            barrier, inc=1, device_id={"chan": (me + step) % devices}, device_id_type=MESH
        )

    def send(src, dst, ssem, rsem, peer):
        return pltpu.make_async_remote_copy(
            src_ref=src,
            dst_ref=dst,
            send_sem=ssem,
            recv_sem=rsem,
            device_id={"chan": peer},
            device_id_type=MESH,
        )

    half = cos_a.shape[0]
    loads[0].wait()
    lane = lax.broadcasted_iota(jnp.int32, (1, LANES), 1)
    quarter = LANES // 4
    group = lane // quarter
    pieces = []
    for piece in range(columns // LANES):
        here = freq_ref[piece // 2 : piece // 2 + 1, :]
        shifts = (2 * quarter, 3 * quarter, 3 * quarter, 0) if piece % 2 else (0, quarter, quarter, 2 * quarter)
        turned = [pltpu.roll(here, n, 1) if n else here for n in shifts]
        pieces.append(
            jnp.where(
                group == 0,
                turned[0],
                jnp.where(group == 1, turned[1], jnp.where(group == 2, turned[2], turned[3])),
            )
        )
    freqs = jnp.concatenate(pieces, axis=1)
    column = lax.broadcasted_iota(jnp.int32, (half, columns), 1)
    row = lax.broadcasted_iota(jnp.int32, (half, columns), 0)
    part_size = columns // devices // 2
    shift = ((column // part_size) & 1) * (samples // 4)
    sin_v, cos_v = sincos_bins(freqs * (row * half) + shift, samples)
    sin_a[...] = sin_v
    cos_a[...] = cos_v
    sin_v, cos_v = sincos_bins(freqs * row, samples)
    sin_b[...] = sin_v
    cos_b[...] = cos_v

    for load in loads[1:4]:
        load.wait()
    owners = [owner_ref[block] for block in range(blocks)]
    shapes = jnp.concatenate([modes_ref[owner] for owner in owners], axis=0)
    inner = lax.dot_general(shapes, shapes, (((1,), (1,)), ((), ())), preferred_element_type=f32)
    low_half = lax.broadcasted_iota(jnp.int32, (modes, LANES), 1) < modes
    for pair in range(blocks // 2):
        base = pair * LANES
        gram_part[pair * modes : (pair + 1) * modes, :] = jnp.where(
            low_half,
            inner[base : base + modes, base : base + LANES],
            inner[base + modes : base + LANES, base : base + LANES],
        )
    pl.semaphore_wait(barrier, devices - 1)

    @pl.loop(1, devices)
    def _(step):
        peer = (me + step) % devices
        send(
            gram_part.at[pl.ds(pl.multiple_of(peer * 8, 8), 8), :],
            gram_recv.at[me],
            gram_ssem.at[peer],
            gram_rsem.at[me],
            peer,
        ).start()

    gram_recv[me] = gram_part[pl.ds(pl.multiple_of(me * 8, 8), 8), :]

    for load in loads[4:]:
        load.wait()
    own_rows = pl.ds(pl.multiple_of(me * 8, 8), 8)
    per_chunk = width // (columns // devices)
    chunk_count = columns // width
    wide_low = lax.broadcasted_iota(jnp.int32, (blocks * modes, LANES), 1) < LANES // 2
    thin_low = wide_low[:8]

    def core_copy(chunk):
        return send(
            core_send.at[chunk], core_recv.at[chunk], core_ssem.at[chunk], core_rsem.at[chunk], other_core
        )

    def side_copy(chunk):
        return send(
            side_send.at[chunk], side_recv.at[chunk], side_ssem.at[chunk], side_rsem.at[chunk], other_side
        )

    def far_copy(chunk, slot):
        peer = chunk * 4 + side * 2 + core
        return send(far_send.at[chunk], far_recv.at[slot], far_ssem.at[chunk], far_rsem.at[slot], peer)

    def chunk_of(step):
        return (far + 1 + step) % chunk_count

    def make(step):
        chunk = chunk_of(step)
        cols = pl.ds(pl.multiple_of(chunk * width, width), width)
        cb = cos_b[:, cols]
        sb = sin_b[:, cols]

        def build(first):
            for a in range(first, first + half // 4):
                ca = cos_a[a : a + 1, cols]
                sa = sin_a[a : a + 1, cols]
                table[a * half : (a + 1) * half, :] = (ca * cb - sa * sb).astype(jnp.bfloat16)

        parts = []
        sums = []
        build(0)
        both = None
        for quart in range(4):
            rows = slice(quart * samples // 4, (quart + 1) * samples // 4)
            term = jnp.dot(snaps[:, rows], table[rows, :], preferred_element_type=f32)
            if quart < 3:
                build((quart + 1) * half // 4)
            both = term if both is None else both + term
        both = both.astype(jnp.bfloat16)
        for snap in range(snap_count):
            spectra = both[snap * channels : (snap + 1) * channels]
            wide = spectra.astype(f32)
            sums.append(jnp.broadcast_to(jnp.sum(wide * wide, axis=0, keepdims=True), (8, width)))
            parts.append(jnp.dot(shapes, spectra, preferred_element_type=f32))
        for pair in range(per_chunk // 2):
            lanes = slice(pair * LANES, (pair + 1) * LANES)
            p0, p1 = parts[0][:, lanes], parts[1][:, lanes]
            t0, t1 = sums[0][:, lanes], sums[1][:, lanes]
            first = jnp.where(wide_low, p0, pltpu.roll(p1, LANES // 2, 1))
            second = jnp.where(wide_low, pltpu.roll(p0, LANES // 2, 1), p1)
            kept[chunk, pair] = jnp.where(core == 0, first, second)
            core_send[chunk, pair] = jnp.where(core == 0, second, first).astype(jnp.bfloat16)
            dest = chunk * per_chunk + 2 * pair
            trace_send[dest] = jnp.where(thin_low, t0, pltpu.roll(t1, LANES // 2, 1))[:1]
            trace_send[dest + 1] = jnp.where(thin_low, pltpu.roll(t0, LANES // 2, 1), t1)[:1]
        core_copy(chunk).start()
        for k in range(per_chunk):
            dest = chunk * per_chunk + k

            @pl.when(dest != me)
            def _():
                send(
                    trace_send.at[dest],
                    trace_recv.at[me],
                    trace_ssem.at[dest],
                    trace_rsem.at[me],
                    dest,
                ).start()

    def add_core(step):
        chunk = chunk_of(step)
        core_copy(chunk).wait_recv()
        side_kept[chunk] = kept[chunk, side] + core_recv[chunk, side].astype(f32)
        side_send[chunk] = (kept[chunk, 1 - side] + core_recv[chunk, 1 - side].astype(f32)).astype(
            jnp.bfloat16
        )
        side_copy(chunk).start()

    def add_side(step, keep=False):
        chunk = chunk_of(step)
        side_copy(chunk).wait_recv()
        total = side_kept[chunk] + side_recv[chunk].astype(f32)
        if keep:
            far_kept[...] = total
        else:
            far_send[chunk] = total.astype(jnp.bfloat16)
            far_copy(chunk, far).start()

    def gram_share():
        @pl.loop(1, devices)
        def _(step):
            peer = (me + step) % devices
            send(
                gram_part.at[pl.ds(0, 8), :],
                gram_recv.at[peer],
                gram_ssem.at[peer],
                gram_rsem.at[peer],
                peer,
            ).wait_recv()

        gram_own[...] = jnp.sum(gram_recv[...], axis=0)
        gram_full[own_rows, :] = gram_own[...]

        @pl.loop(1, devices)
        def _(step):
            peer = (me + step) % devices
            send(
                gram_own, gram_full.at[own_rows, :], full_ssem.at[peer], full_rsem.at[me], peer
            ).start()

    last = chunk_count - 1

    @pl.loop(0, chunk_count)
    def _(step):
        make(step)

        @pl.when(step == 0)
        def _():
            gram_share()

        @pl.when(step >= 1)
        def _():
            add_core(step - 1)

        @pl.when(step >= 2)
        def _():
            add_side(step - 2)

    trace_recv[me] = trace_send[me]

    @pl.loop(1, devices)
    def _(step):
        peer = (me + step) % devices
        send(
            gram_own,
            gram_full.at[pl.ds(pl.multiple_of(peer * 8, 8), 8), :],
            full_ssem.at[peer],
            full_rsem.at[peer],
            peer,
        ).wait_recv()

    gram = gram_full[...].astype(jnp.bfloat16).astype(f32)
    tile = 16
    first_tile = (lax.broadcasted_iota(jnp.int32, gram.shape, 0) % modes) // tile
    second_tile = (lax.broadcasted_iota(jnp.int32, gram.shape, 1) % modes) // tile
    gram = jnp.where(first_tile > second_tile, 2.0 * gram, gram)
    pairs = sum(tile * (modes - start) for start in range(0, modes, tile))
    wide_lane = lax.broadcasted_iota(jnp.int32, (modes, LANES), 1)
    mode_ids = lax.broadcasted_iota(jnp.int32, (modes, depths), 0)
    sources = []
    waves_sin = []
    waves_cos = []
    norms = []
    for block in range(blocks):
        if block == 1:
            add_core(last)
            add_side(last - 1)
        wave = waves_ref[owners[block]]
        wave = jnp.where(wide_lane // quarter == me % 4, wave, 0.0)
        wave = wave + pltpu.roll(wave, quarter, 1)
        wave = wave + pltpu.roll(wave, 2 * quarter, 1)
        range_ids = block * RPB + wide_lane // quarter
        phases = wave * (range_start + range_step * range_ids.astype(f32))
        sine, cosine = sincos_wide(phases)
        scale = 1.0 / jnp.sqrt(phases)
        sine, cosine = sine * scale, cosine * scale
        waves_sin.append(sine)
        waves_cos.append(cosine)
        source = jnp.where(
            mode_ids < counts_ref[owners[block]], modes_source_ref[owners[block]], 0.0
        )
        sources.append(source)
        base = (block // 2) * modes
        filled = 0
        for m in range(modes):
            low = m // tile * tile
            lane = (block % 2) * modes + m
            at = slice(filled, filled + modes - low)
            filled += modes - low
            terms_a[at, :] = (
                cosine[m : m + 1] * cosine[low:] + sine[m : m + 1] * sine[low:]
            ).astype(jnp.bfloat16)
            terms_b[at, :] = (
                gram[base + low : base + modes, lane : lane + 1] * (source[m : m + 1] * source[low:])
            ).astype(jnp.bfloat16)
        norms.append(
            lax.dot_general(
                terms_a[:pairs],
                terms_b[:pairs],
                (((0,), (0,)), ((), ())),
                preferred_element_type=f32,
            )
        )

    add_side(last, keep=True)

    @pl.loop(1, devices)
    def _(step):
        peer = (me + step) % devices
        send(
            trace_send.at[peer],
            trace_recv.at[peer],
            trace_ssem.at[peer],
            trace_rsem.at[peer],
            peer,
        ).wait_recv()

    proj = far_kept[...]
    for step in range(1, chunk_count):
        slot = (far + step) % chunk_count
        far_copy(slot, slot).wait_recv()
        proj = proj + far_recv[slot].astype(f32)
    proj = proj.astype(jnp.bfloat16)
    trace = jnp.broadcast_to(jnp.sum(trace_recv[...], axis=0), (8, LANES))
    trace = trace + pltpu.roll(trace, 2 * quarter, 1)
    trace = trace + pltpu.roll(trace, quarter, 1)
    level = (1.0 / jnp.sqrt(snap_count * trace))[:1]

    pick_in = lax.broadcasted_iota(jnp.int32, (LANES, 4 * LANES), 0)
    pick_out = lax.broadcasted_iota(jnp.int32, (LANES, 4 * LANES), 1)
    pick = (pick_in // quarter == pick_out // LANES) & (pick_in % quarter == pick_out % quarter)
    spread = jnp.dot(proj, pick.astype(f32).astype(jnp.bfloat16), preferred_element_type=f32)
    for block in range(blocks):
        sine, cosine = waves_sin[block] * level, waves_cos[block] * level
        rows = slice(block * modes, (block + 1) * modes)
        coupled = []
        for snap in range(snap_count):
            real = spread[rows, (2 * snap) * LANES : (2 * snap + 1) * LANES]
            imag = spread[rows, (2 * snap + 1) * LANES : (2 * snap + 2) * LANES]
            coupled.append(cosine * real + sine * imag)
            coupled.append(cosine * imag - sine * real)
        coupled = jnp.concatenate(coupled, axis=1)
        coupled_high = coupled.astype(jnp.bfloat16)
        coupled_low = (coupled - coupled_high.astype(f32)).astype(jnp.bfloat16)
        source = sources[block]
        source_high = source.astype(jnp.bfloat16)
        source_low = (source - source_high.astype(f32)).astype(jnp.bfloat16)
        beams = lax.dot_general(
            jnp.concatenate([coupled_high, coupled_low, coupled_high], axis=0),
            jnp.concatenate([source_high, source_high, source_low], axis=0),
            (((0,), (0,)), ((), ())),
            preferred_element_type=f32,
        )
        squares = beams * beams
        power = (
            squares[:LANES]
            + squares[LANES : 2 * LANES]
            + squares[2 * LANES : 3 * LANES]
            + squares[3 * LANES :]
        )
        ratio = power / norms[block]
        for j in range(4):
            surf_own[block * 4 + j : block * 4 + j + 1, :] = jnp.sum(
                ratio[j * quarter : (j + 1) * quarter], axis=0, keepdims=True
            )

    surf_recv[me] = surf_own[...]

    @pl.loop(1, devices)
    def _(step):
        peer = (me + step) % devices
        send(surf_own, surf_recv.at[me], surf_ssem.at[peer], surf_rsem.at[me], peer).start()

    @pl.loop(1, devices)
    def _(step):
        peer = (me + step) % devices
        send(
            gram_part.at[pl.ds(pl.multiple_of(peer * 8, 8), 8), :],
            gram_recv.at[me],
            gram_ssem.at[peer],
            gram_rsem.at[me],
            peer,
        ).wait_send()
        send(
            gram_own, gram_full.at[own_rows, :], full_ssem.at[peer], full_rsem.at[me], peer
        ).wait_send()
        send(
            trace_send.at[peer], trace_recv.at[me], trace_ssem.at[peer], trace_rsem.at[me], peer
        ).wait_send()

    @pl.loop(0, chunk_count)
    def _(chunk):
        core_copy(chunk).wait_send()
        side_copy(chunk).wait_send()

        @pl.when(chunk != far)
        def _():
            far_copy(chunk, far).wait_send()

    @pl.loop(1, devices)
    def _(step):
        peer = (me + step) % devices
        send(surf_own, surf_recv.at[peer], surf_ssem.at[peer], surf_rsem.at[peer], peer).wait()

    total = jnp.sum(surf_recv[...], axis=0) / (columns // 2)
    total_ref[...] = total
    out_ref[...] = total_ref[pl.ds(me, 1), :] / jnp.max(total)


def per_device_fused(
    snapshots, freq_bins, mode_shapes, mode_counts, wavenumbers, source_modes, segment_owner
):
    devices = lax.axis_size("chan")
    snap_count, channels, samples = snapshots.shape
    segs, modes, depths = source_modes.shape
    blocks = segment_owner.shape[0]
    freqs = freq_bins.shape[0]
    columns = 2 * freqs
    half = math.isqrt(samples)
    rows = blocks * modes
    f32, bf16 = jnp.float32, jnp.bfloat16
    ranges_total = blocks * RPB
    dma = pltpu.SemaphoreType.DMA((devices,))
    vmem = pl.BlockSpec(memory_space=pltpu.VMEM)
    few = pltpu.SemaphoreType.DMA((devices // 4,))
    return pl.pallas_call(
        functools.partial(fused_kernel, devices),
        out_shape=jax.ShapeDtypeStruct((1, depths), f32),
        in_specs=[pl.BlockSpec(memory_space=pltpu.HBM)] * 7,
        out_specs=vmem,
        scratch_shapes=[
            pltpu.VMEM((freqs // LANES, LANES), jnp.int32),
            pltpu.VMEM((segs, modes, channels), bf16),
            pltpu.SMEM((segs,), jnp.int32),
            pltpu.VMEM((segs, modes, LANES), f32),
            pltpu.VMEM((segs, modes, depths), f32),
            pltpu.SMEM((blocks,), jnp.int32),
            pltpu.VMEM((snap_count * channels, samples), bf16),
            pltpu.VMEM((samples, 256), bf16),
            pltpu.VMEM((half, columns), f32),
            pltpu.VMEM((half, columns), f32),
            pltpu.VMEM((half, columns), f32),
            pltpu.VMEM((half, columns), f32),
            pltpu.VMEM((devices // 4, 2, rows, LANES), f32),
            pltpu.VMEM((devices // 4, 2, rows, LANES), bf16),
            pltpu.VMEM((devices // 4, 2, rows, LANES), bf16),
            pltpu.VMEM((devices // 4, rows, LANES), f32),
            pltpu.VMEM((devices // 4, rows, LANES), bf16),
            pltpu.VMEM((devices // 4, rows, LANES), bf16),
            pltpu.VMEM((rows, LANES), f32),
            pltpu.VMEM((devices // 4, rows, LANES), bf16),
            pltpu.VMEM((devices // 4, rows, LANES), bf16),
            pltpu.VMEM((devices, 1, LANES), f32),
            pltpu.VMEM((devices, 1, LANES), f32),
            pltpu.VMEM((devices * 8, LANES), f32),
            pltpu.VMEM((devices, 8, LANES), f32),
            pltpu.VMEM((8, LANES), f32),
            pltpu.VMEM((devices * 8, LANES), f32),
            pltpu.VMEM((modes * modes, LANES), bf16),
            pltpu.VMEM((modes * modes, LANES), bf16),
            pltpu.VMEM((ranges_total, depths), f32),
            pltpu.VMEM((devices, ranges_total, depths), f32),
            pltpu.VMEM((ranges_total, depths), f32),
            pltpu.SemaphoreType.DMA((7,)),
        ]
        + [few] * 6
        + [dma] * 8,
        compiler_params=pltpu.CompilerParams(
            collective_id=0, has_side_effects=True, vmem_limit_bytes=62 * 2**20
        ),
    )(
        freq_bins.reshape(freqs // LANES, LANES),
        snapshots.reshape(snap_count * channels, samples),
        mode_shapes,
        mode_counts,
        wavenumbers,
        source_modes,
        segment_owner,
    )


def per_device(*args):
    snapshots, freq_bins, mode_shapes, _, _, source_modes, segment_owner = args
    devices = lax.axis_size("chan")
    blocks = segment_owner.shape[0]
    freqs = freq_bins.shape[0]
    modes, depths = source_modes.shape[1:]
    fits = (
        snapshots.shape[0] == 2
        and 2 * 2 * freqs == devices * LANES
        and 4 * freqs // devices == LANES
        and blocks * RPB == devices
        and blocks * modes * modes == devices * 8 * LANES
        and 2 * modes == LANES
        and depths == LANES
        and math.isqrt(snapshots.shape[2]) ** 2 == snapshots.shape[2]
    )
    return per_device_fused(*args) if fits else per_device_plain(*args)


def solution(mesh):
    return jax.shard_map(
        per_device,
        mesh=mesh,
        in_specs=(P("groups", "chan", None), P(), P(None, None, "chan"), P(), P(), P(), P()),
        out_specs=P(("groups", "chan"), None),
        check_vma=False,
    )
```
